32 devices in a mesh: gx: 4 (over z), gy: 4 (over y, x), gz: 2 (over core).
Axes of the slice: x: 2, y: 2, z: 4, core: 2. Of those that a mesh axis runs over, the one named last changes fastest.
Arguments:
- populations: float32 [19, 16, 64, 256], P(None, 'gx', 'gy', 'gz'), may hold values from 0 to 0.2
- solid: int32 [16, 64, 256], P('gx', 'gy', 'gz'), may hold values 0 or 1
- rates: float32 [19], replicated, may hold values from 0.3 to 1.95
Outputs:
- evolved: float32 [19, 16, 64, 256], P(None, 'gx', 'gy', 'gz')
The draws below stay inside these ranges and needn't reach their ends.
Inputs may be any that keep to these rules, and one draw needn't show every extreme that they name: solid holds only 0 and 1.
All inputs are finite; a program needn't handle non-finite values. No bound on the sum of `solid` on one device may be relied on, other than what follows from the above.
Results may differ from the reference program's by a relative error of at most 0.00011.
Values sent between devices are 32-bit elements; how exact they have to be, the bound alone decides.
A program may use at most 64 MiB of HBM per device.

```python
import math
import jax
import jax.numpy as jnp
import numpy as np
from jax import lax

STEPS = 3
NX = 16
NY = 64
NZ = 256


def set_ends(values, rng, low, largest):
    longest = values.shape.index(max(values.shape))
    spots = []
    for shift in (0, 1):
        where = [jax.random.randint(jax.random.fold_in(rng, axis), (), 0, length) for axis, length in enumerate(values.shape)]
        where[longest] = (where[longest] + shift) % values.shape[longest]
        spots.append(tuple(where))
    return values.at[spots[0]].set(low).at[spots[1]].set(largest)


def levels(own_key, extent, cuts, smallest, top_value):
    def one(position, shards_of):
        steps = jax.random.uniform(jax.random.fold_in(jax.random.fold_in(own_key, 6), position), (shards_of,), jnp.float32, smallest / len(cuts), top_value / len(cuts))
        return jnp.repeat(jnp.exp(steps), extent[position] // shards_of).reshape((-1,) + (1,) * (len(extent) - position - 1))

    level = one(*cuts[0])
    for cut in cuts[1:]:
        level = level * one(*cut)
    return level


def setup_inputs(seed: int = 0) -> dict:
    splits = jax.random.split(jax.random.key(seed), 4)
    return {
        "populations": jnp.clip(0.2 * jax.random.uniform(splits[0], (19, NX, NY, NZ), jnp.float32) ** levels(splits[0], (19, NX, NY, NZ), ((1, 4), (2, 4), (3, 2)), -0.2, 0.2), 0.0, 0.2),
        "solid": set_ends((jax.random.randint(splits[1], (NX, NY, NZ), 0, 4) < 1).astype(jnp.int32), jax.random.fold_in(splits[1], 1), 0, 1),
        "rates": jnp.clip(jnp.exp(jax.random.uniform(splits[2], (19,), jnp.float32, math.log(0.3), math.log(1.95))), 0.3, 1.95),
    }


def invert_table(matrix):
    dimension = matrix.shape[0]
    augmented = np.concatenate([matrix, np.eye(dimension)], axis=1)
    for column in range(dimension):
        pivot_row = column + int(np.argmax(np.abs(augmented[column:, column])))
        augmented[[column, pivot_row]] = augmented[[pivot_row, column]]
        augmented[column] = augmented[column] / augmented[column, column]
        for target_row in range(dimension):
            if target_row != column:
                augmented[target_row] = augmented[target_row] - augmented[target_row, column] * augmented[column]
    return augmented[:, dimension:]


def tables():
    velocity = np.array([[0, 0, 0], [1, 0, 0], [-1, 0, 0], [0, 1, 0], [0, -1, 0], [0, 0, 1], [0, 0, -1],
                         [1, 1, 0], [-1, -1, 0], [1, -1, 0], [-1, 1, 0],
                         [1, 0, 1], [-1, 0, -1], [1, 0, -1], [-1, 0, 1],
                         [0, 1, 1], [0, -1, -1], [0, 1, -1], [0, -1, 1]])
    weights = np.array([1.0 / 3.0] + [1.0 / 18.0] * 6 + [1.0 / 36.0] * 12)
    exponents = [(0, 0, 0), (1, 0, 0), (0, 1, 0), (0, 0, 1), (2, 0, 0), (0, 2, 0), (0, 0, 2),
                 (1, 1, 0), (1, 0, 1), (0, 1, 1), (2, 1, 0), (2, 0, 1), (1, 2, 0), (0, 2, 1),
                 (1, 0, 2), (0, 1, 2), (2, 2, 0), (2, 0, 2), (0, 2, 2)]
    moments = np.array([[1.0 * (int(vel_row[0]) ** power[0] * int(vel_row[1]) ** power[1] * int(vel_row[2]) ** power[2])
                         for vel_row in velocity] for power in exponents])
    inverse = invert_table(moments)
    opposite = [0, 2, 1, 4, 3, 6, 5, 8, 7, 10, 9, 12, 11, 14, 13, 16, 15, 18, 17]
    return velocity, weights, moments, inverse, opposite


def collide(populations, rates):
    velocity, weights, moments, inverse, opposite = tables()
    grid_shape = populations.shape
    columns = populations.reshape(19, -1)
    highest = lax.Precision.HIGHEST
    density = jnp.sum(columns, axis=0)
    momentum = jnp.dot(jnp.asarray(velocity.T, jnp.float32), columns, precision=highest)
    projected = jnp.dot(jnp.asarray(velocity, jnp.float32), momentum, precision=highest)
    momentum_sq = jnp.sum(momentum * momentum, axis=0)
    equilibrium = jnp.asarray(weights, jnp.float32)[:, None] * (
        density + 3.0 * projected + 4.5 * projected * projected - 1.5 * momentum_sq)
    kernel = jnp.dot(jnp.asarray(inverse, jnp.float32), rates[:, None] * jnp.asarray(moments, jnp.float32),
                     precision=highest)
    relaxed = columns - jnp.dot(kernel, columns - equilibrium, precision=highest)
    return relaxed.reshape(grid_shape)


def reference(populations, solid, rates):
    velocity, weights, moments, inverse, opposite = tables()
    for time_step in range(STEPS):
        relaxed = collide(populations, rates)
        outputs = []
        for index in range(19):
            offset = (int(velocity[index][0]), int(velocity[index][1]), int(velocity[index][2]))
            source = jnp.roll(relaxed[index], offset, axis=(0, 1, 2))
            blocked = jnp.roll(solid, offset, axis=(0, 1, 2))
            value = jnp.where(blocked == 1, relaxed[opposite[index]], source)
            outputs.append(jnp.where(solid == 1, 0.0, value))
        populations = jnp.stack(outputs)
    return populations
```

```python
import functools

import jax
import jax.numpy as jnp
from jax import lax
from jax.experimental import pallas as pl
from jax.experimental.pallas import tpu as pltpu
from jax.sharding import PartitionSpec as P

STEPS = 3
VELOCITY = [
    (0, 0, 0), (1, 0, 0), (-1, 0, 0), (0, 1, 0), (0, -1, 0), (0, 0, 1), (0, 0, -1),
    (1, 1, 0), (-1, -1, 0), (1, -1, 0), (-1, 1, 0),
    (1, 0, 1), (-1, 0, -1), (1, 0, -1), (-1, 0, 1),
    (0, 1, 1), (0, -1, -1), (0, 1, -1), (0, -1, 1),
]
OPPOSITE = [0, 2, 1, 4, 3, 6, 5, 8, 7, 10, 9, 12, 11, 14, 13, 16, 15, 18, 17]
X_OUT = ([1, 7, 9, 11, 13], [2, 8, 10, 12, 14])
Y_OUT = ([3, 7, 10, 15, 17], [4, 8, 9, 16, 18])
EDGE = [7, 8, 9, 10]
MESH = pl.DeviceIdType.MESH


def collide(f, rate):
    pairs = [(index, index + 1) for index in range(1, 19, 2)]
    total = [f[a] + f[b] for a, b in pairs]
    diff = [f[a] - f[b] for a, b in pairs]
    density = f[0] + ((total[0] + total[1] + total[2]) + (total[3] + total[4])
                      + (total[5] + total[6]) + (total[7] + total[8]))
    jx = diff[0] + (diff[3] + diff[4]) + (diff[5] + diff[6])
    jy = diff[1] + (diff[3] - diff[4]) + (diff[7] + diff[8])
    jz = diff[2] + (diff[5] - diff[6]) + (diff[7] - diff[8])
    base = density - 1.5 * (jx * jx + jy * jy + jz * jz)
    projected = [jx, jy, jz, jx + jy, jx - jy, jx + jz, jx - jz, jy + jz, jy - jz]
    rest = f[0] - (1.0 / 3.0) * base
    even, odd = [], []
    for k in range(9):
        weight = 1.0 / 18.0 if k < 3 else 1.0 / 36.0
        p = projected[k]
        even.append(total[k] - (2.0 * weight) * (base + 4.5 * (p * p)))
        odd.append(diff[k] - (6.0 * weight) * p)
    xxyy, xxzz, yyzz = even[3] + even[4], even[5] + even[6], even[7] + even[8]
    xyy, xzz, yzz = odd[3] + odd[4], odd[5] + odd[6], odd[7] + odd[8]
    xxy, xxz, yyz = odd[3] - odd[4], odd[5] - odd[6], odd[7] - odd[8]
    one = rate[0] * (rest + ((even[0] + even[1] + even[2]) + (xxyy + xxzz + yyzz)))
    mx = rate[1] * (odd[0] + xyy + xzz)
    my = rate[2] * (odd[1] + xxy + yzz)
    mz = rate[3] * (odd[2] + xxz + yyz)
    xx = rate[4] * (even[0] + xxyy + xxzz)
    yy = rate[5] * (even[1] + xxyy + yyzz)
    zz = rate[6] * (even[2] + xxzz + yyzz)
    xy = rate[7] * (even[3] - even[4])
    xz = rate[8] * (even[5] - even[6])
    yz = rate[9] * (even[7] - even[8])
    xxy, xxz, xyy = rate[10] * xxy, rate[11] * xxz, rate[12] * xyy
    yyz, xzz, yzz = rate[13] * yyz, rate[14] * xzz, rate[15] * yzz
    xxyy, xxzz, yyzz = rate[16] * xxyy, rate[17] * xxzz, rate[18] * yyzz
    change = [None] * 19
    change[0] = one - (xx + yy + zz) + (xxyy + xxzz + yyzz)
    sums = [xx - xxyy - xxzz, yy - xxyy - yyzz, zz - xxzz - yyzz]
    diffs = [mx - xyy - xzz, my - xxy - yzz, mz - xxz - yyz]
    for k in range(3):
        change[1 + 2 * k] = 0.5 * (sums[k] + diffs[k])
        change[2 + 2 * k] = 0.5 * (sums[k] - diffs[k])
    for k, (s, d, a, b) in enumerate(
        [(xxyy, xy, xyy, xxy), (xxzz, xz, xzz, xxz), (yyzz, yz, yzz, yyz)]
    ):
        plus, minus = 0.25 * (s + d), 0.25 * (s - d)
        up, down = 0.25 * (a + b), 0.25 * (a - b)
        change[7 + 4 * k] = plus + up
        change[8 + 4 * k] = plus - up
        change[9 + 4 * k] = minus + down
        change[10 + 4 * k] = minus - down
    return [f[index] - change[index] for index in range(19)]


def kernel(sizes, pop, sol, rates, out, held, relaxed, flag, blocked, xs, xr, ys, yr, es, er,
           osend, iflag, own_sem, in_send, in_recv, x_send, x_recv, y_send, y_recv, e_send, e_recv,
           o_send, o_recv):
    gxn, gyn, gzn, nx, ny = sizes
    pair = gzn == 2
    gx, gy, gz = lax.axis_index("gx"), lax.axis_index("gy"), lax.axis_index("gz")
    row_block = gy * gzn + gz

    def device(dx, dy):
        block = lax.rem(row_block + dy + gyn * gzn, gyn * gzn)
        return (lax.rem(gx + dx + gxn, gxn), block // gzn, lax.rem(block, gzn))

    order = [0, nx - 1] + list(range(1, nx - 1))
    local = []
    if pair:
        other = (gx, gy, 1 - gz)
        mine = pl.ds(pl.multiple_of(gz * ny, ny), ny)
        others = pl.ds(pl.multiple_of((1 - gz) * ny, ny), ny)
        for x in order:
            local.append(pltpu.make_async_copy(
                pop.at[:, x, mine, :], held.at[:, x, gz], own_sem.at[x]))
        local.append(pltpu.make_async_copy(sol.at[:, mine, :], iflag.at[:, gz], own_sem.at[nx]))
    else:
        for x in order:
            local.append(pltpu.make_async_copy(pop.at[:, x], held.at[:, x], own_sem.at[x]))
        local.append(pltpu.make_async_copy(sol, iflag, own_sem.at[nx]))
    for copy in local:
        copy.start()

    barrier = pltpu.get_barrier_semaphore()
    around = [(dx, dy) for dx in (-1, 0, 1) for dy in (-1, 0, 1) if (dx, dy) != (0, 0)]
    for dx, dy in around:
        pl.semaphore_signal(barrier, inc=1, device_id=device(dx, dy), device_id_type=MESH)
    pl.semaphore_wait(barrier, len(around))

    def remote(src, dst, send, recv, to):
        copy = pltpu.make_async_remote_copy(
            src_ref=src, dst_ref=dst, send_sem=send, recv_sem=recv,
            device_id=to, device_id_type=MESH)
        copy.start()
        return copy

    moved = []
    if pair:
        for x in order:
            moved.append(remote(pop.at[:, x, others, :], held.at[:, x, gz],
                                in_send.at[x], in_recv.at[x], other))
        moved.append(remote(sol.at[:, others, :], iflag.at[:, gz],
                            in_send.at[nx], in_recv.at[nx], other))

    shape = (gzn, ny, 128)
    row = lax.broadcasted_iota(jnp.int32, shape, 1)
    lane = lax.broadcasted_iota(jnp.int32, shape, 2)
    rate = [rates[index] for index in range(19)]
    sent = list(moved)

    def arrived(index):
        local[index].wait()
        if pair:
            moved[index].wait_recv()

    def shifted(plane, halo, velocity):
        cx, cy, cz = velocity
        value = plane()
        if cy:
            value = jnp.where(row == (0 if cy > 0 else ny - 1),
                              jnp.broadcast_to(halo(), shape), pltpu.roll(value, cy % ny, 1))
        if cz:
            turned = pltpu.roll(value, cz % 128, 2)
            if cz > 0:
                swapped = jnp.concatenate([turned[-1:], turned[:-1]], axis=0)
            else:
                swapped = jnp.concatenate([turned[1:], turned[:1]], axis=0)
            value = jnp.where(lane == (0 if cz > 0 else 127), swapped, turned)
        return value

    def source(t, p, x, is_flag):
        cx, cy, cz = VELOCITY[p]
        sx = x - cx
        outside = sx < 0 or sx >= nx
        xd, yd = (0 if cx > 0 else 1), (0 if cy > 0 else 1)

        def plane():
            if outside:
                return xr[t, xd, 5 if is_flag else X_OUT[xd].index(p)]
            return flag[sx] if is_flag else relaxed[p, sx]

        def halo():
            if outside:
                return er[t, EDGE.index(p), 1 if is_flag else 0]
            return yr[t, yd, 5 if is_flag else Y_OUT[yd].index(p), sx]

        return shifted(plane, halo, (cx, cy, cz))

    for t in range(STEPS):
        last = t == STEPS - 1
        if t == 0:
            arrived(nx)
            for x in range(nx):
                flag[x] = iflag[x].astype(jnp.float32)
                for d, at in ((0, ny - 1), (1, 0)):
                    ys[0, d, 5, x] = flag[x, :, at : at + 1, :]
            xs[0, 0, 5] = flag[nx - 1]
            xs[0, 1, 5] = flag[0]
            for e, p in enumerate(EDGE):
                cx, cy, _ = VELOCITY[p]
                at = ny - 1 if cy > 0 else 0
                es[0, e, 1] = flag[nx - 1 if cx > 0 else 0, :, at : at + 1, :]
        count = 6 if t == 0 else 5
        ecount = 2 if t == 0 else 1
        x_copies, e_copies, y_copies = [], [], []
        for place, x in enumerate(order):
            if t == 0:
                arrived(place)
            values = collide([held[index, x] for index in range(19)], rate)
            for index in range(19):
                relaxed[index, x] = values[index]
            for d, at in ((0, ny - 1), (1, 0)):
                for k, p in enumerate(Y_OUT[d]):
                    ys[t, d, k, x] = values[p][:, at : at + 1, :]
            d = {nx - 1: 0, 0: 1}.get(x)
            if d is not None:
                for k, p in enumerate(X_OUT[d]):
                    xs[t, d, k] = values[p]
                x_copies.append(remote(
                    xs.at[t, d, pl.ds(0, count)], xr.at[t, d, pl.ds(0, count)],
                    x_send.at[t, d], x_recv.at[t, d], device(1 if d == 0 else -1, 0)))
                for e, p in enumerate(EDGE):
                    cx, cy, _ = VELOCITY[p]
                    if (cx > 0) == (d == 0):
                        at = ny - 1 if cy > 0 else 0
                        es[t, e, 0] = values[p][:, at : at + 1, :]
                        e_copies.append(remote(
                            es.at[t, e, pl.ds(0, ecount)], er.at[t, e, pl.ds(0, ecount)],
                            e_send.at[t, e], e_recv.at[t, e], device(cx, cy)))
        for d in (0, 1):
            y_copies.append(remote(
                ys.at[t, d, pl.ds(0, count)], yr.at[t, d, pl.ds(0, count)],
                y_send.at[t, d], y_recv.at[t, d], device(0, 1 if d == 0 else -1)))
        sent += x_copies + e_copies + y_copies
        for copy in y_copies:
            copy.wait_recv()
        for place, x in enumerate(order[2:] + order[:2]):
            if place == nx - 2:
                for copy in x_copies + e_copies:
                    copy.wait_recv()
            rock = flag[x] > 0.5
            for p in range(19):
                if p == 0:
                    value = relaxed[0, x]
                else:
                    if t == 0:
                        wall = source(0, p, x, True)
                        blocked[p, x] = wall
                    else:
                        wall = blocked[p, x]
                    value = jnp.where(wall > 0.5, relaxed[OPPOSITE[p], x], source(t, p, x, False))
                value = jnp.where(rock, 0.0, value)
                if not last:
                    held[p, x] = value
                elif pair:
                    first = gz == 0
                    out[p, x, mine, :] = jnp.where(first, value[0], value[1])
                    osend[p, x] = jnp.where(first, value[1], value[0])
                else:
                    out[p, x] = value
            if last and pair:
                copy = remote(osend.at[:, x], out.at[:, x, mine, :],
                              o_send.at[x], o_recv.at[x], other)
                sent.append(copy)
                moved.append(copy)
    if pair:
        for copy in moved[nx + 1:]:
            copy.wait_recv()
    for copy in sent:
        copy.wait_send()


def shards(sizes, populations, solid, rates):
    gxn, gyn, gzn, nx, ny = sizes
    pair = gzn == 2
    if not pair:
        populations = lax.all_to_all(
            populations.reshape(19, nx, gzn, ny, 128), "gz", 2, 2, tiled=True)
        solid = lax.all_to_all(solid.reshape(nx, gzn, ny, 128), "gz", 1, 1, tiled=True)
    f32, dma, vmem = jnp.float32, pltpu.SemaphoreType.DMA, pltpu.VMEM
    block = (gzn, ny, 128)
    line = (gzn, 1, 128)
    out = pl.pallas_call(
        functools.partial(kernel, sizes),
        out_shape=jax.ShapeDtypeStruct(populations.shape, f32),
        in_specs=[
            pl.BlockSpec(memory_space=pl.ANY),
            pl.BlockSpec(memory_space=pl.ANY),
            pl.BlockSpec(memory_space=pltpu.SMEM),
        ],
        out_specs=pl.BlockSpec(memory_space=pltpu.VMEM),
        scratch_shapes=[
            vmem((19, nx) + block, f32),
            vmem((19, nx) + block, f32),
            vmem((nx,) + block, f32),
            vmem((19, nx) + block, f32),
            vmem((STEPS, 2, 6) + block, f32),
            vmem((STEPS, 2, 6) + block, f32),
            vmem((STEPS, 2, 6, nx) + line, f32),
            vmem((STEPS, 2, 6, nx) + line, f32),
            vmem((STEPS, 4, 2) + line, f32),
            vmem((STEPS, 4, 2) + line, f32),
            vmem((19, nx, ny, 128), f32),
            vmem((nx,) + block, jnp.int32),
            dma((nx + 1,)),
            dma((nx + 1,)),
            dma((nx + 1,)),
            dma((STEPS, 2)),
            dma((STEPS, 2)),
            dma((STEPS, 2)),
            dma((STEPS, 2)),
            dma((STEPS, 4)),
            dma((STEPS, 4)),
            dma((nx,)),
            dma((nx,)),
        ],
        compiler_params=pltpu.CompilerParams(
            collective_id=0, has_side_effects=True, vmem_limit_bytes=32 * 1024 * 1024),
    )(populations, solid, rates)
    if not pair:
        out = lax.all_to_all(out, "gz", 2, 2, tiled=True).reshape(19, nx, gzn * ny, 128)
    return out


def solution(mesh):
    gxn, gyn, gzn = mesh.shape["gx"], mesh.shape["gy"], mesh.shape["gz"]

    def run(populations, solid, rates):
        sizes = (gxn, gyn, gzn, populations.shape[1] // gxn, populations.shape[2] // (gyn * gzn))
        in_specs = (P(None, "gx", "gy", "gz"), P("gx", "gy", "gz"), P())
        out_specs = P(None, "gx", "gy", "gz")
        return jax.shard_map(functools.partial(shards, sizes), mesh=mesh, in_specs=in_specs,
                             out_specs=out_specs, check_vma=False)(populations, solid, rates)

    return run
```

```python
import functools

import jax
import jax.numpy as jnp
from jax import lax
from jax.experimental import pallas as pl
from jax.experimental.pallas import tpu as pltpu
from jax.sharding import PartitionSpec as P

STEPS = 3
VELOCITY = [
    (0, 0, 0), (1, 0, 0), (-1, 0, 0), (0, 1, 0), (0, -1, 0), (0, 0, 1), (0, 0, -1),
    (1, 1, 0), (-1, -1, 0), (1, -1, 0), (-1, 1, 0),
    (1, 0, 1), (-1, 0, -1), (1, 0, -1), (-1, 0, 1),
    (0, 1, 1), (0, -1, -1), (0, 1, -1), (0, -1, 1),
]
OPPOSITE = [0, 2, 1, 4, 3, 6, 5, 8, 7, 10, 9, 12, 11, 14, 13, 16, 15, 18, 17]
X_OUT = ([1, 7, 9, 11, 13], [2, 8, 10, 12, 14])
Y_OUT = ([3, 7, 10, 15, 17], [4, 8, 9, 16, 18])
EDGE = [7, 8, 9, 10]
MESH = pl.DeviceIdType.MESH


def collide(f, rate):
    pairs = [(index, index + 1) for index in range(1, 19, 2)]
    total = [f[a] + f[b] for a, b in pairs]
    diff = [f[a] - f[b] for a, b in pairs]
    density = f[0] + ((total[0] + total[1] + total[2]) + (total[3] + total[4])
                      + (total[5] + total[6]) + (total[7] + total[8]))
    jx = diff[0] + (diff[3] + diff[4]) + (diff[5] + diff[6])
    jy = diff[1] + (diff[3] - diff[4]) + (diff[7] + diff[8])
    jz = diff[2] + (diff[5] - diff[6]) + (diff[7] - diff[8])
    base = density - 1.5 * (jx * jx + jy * jy + jz * jz)
    projected = [jx, jy, jz, jx + jy, jx - jy, jx + jz, jx - jz, jy + jz, jy - jz]
    rest = f[0] - (1.0 / 3.0) * base
    even, odd = [], []
    for k in range(9):
        weight = 1.0 / 18.0 if k < 3 else 1.0 / 36.0
        p = projected[k]
        even.append(total[k] - (2.0 * weight) * (base + 4.5 * (p * p)))
        odd.append(diff[k] - (6.0 * weight) * p)
    xxyy, xxzz, yyzz = even[3] + even[4], even[5] + even[6], even[7] + even[8]
    xyy, xzz, yzz = odd[3] + odd[4], odd[5] + odd[6], odd[7] + odd[8]
    xxy, xxz, yyz = odd[3] - odd[4], odd[5] - odd[6], odd[7] - odd[8]
    one = rate[0] * (rest + ((even[0] + even[1] + even[2]) + (xxyy + xxzz + yyzz)))
    mx = rate[1] * (odd[0] + xyy + xzz)
    my = rate[2] * (odd[1] + xxy + yzz)
    mz = rate[3] * (odd[2] + xxz + yyz)
    xx = rate[4] * (even[0] + xxyy + xxzz)
    yy = rate[5] * (even[1] + xxyy + yyzz)
    zz = rate[6] * (even[2] + xxzz + yyzz)
    xy = rate[7] * (even[3] - even[4])
    xz = rate[8] * (even[5] - even[6])
    yz = rate[9] * (even[7] - even[8])
    xxy, xxz, xyy = rate[10] * xxy, rate[11] * xxz, rate[12] * xyy
    yyz, xzz, yzz = rate[13] * yyz, rate[14] * xzz, rate[15] * yzz
    xxyy, xxzz, yyzz = rate[16] * xxyy, rate[17] * xxzz, rate[18] * yyzz
    change = [None] * 19
    change[0] = one - (xx + yy + zz) + (xxyy + xxzz + yyzz)
    sums = [xx - xxyy - xxzz, yy - xxyy - yyzz, zz - xxzz - yyzz]
    diffs = [mx - xyy - xzz, my - xxy - yzz, mz - xxz - yyz]
    for k in range(3):
        change[1 + 2 * k] = 0.5 * (sums[k] + diffs[k])
        change[2 + 2 * k] = 0.5 * (sums[k] - diffs[k])
    for k, (s, d, a, b) in enumerate(
        [(xxyy, xy, xyy, xxy), (xxzz, xz, xzz, xxz), (yyzz, yz, yzz, yyz)]
    ):
        plus, minus = 0.25 * (s + d), 0.25 * (s - d)
        up, down = 0.25 * (a + b), 0.25 * (a - b)
        change[7 + 4 * k] = plus + up
        change[8 + 4 * k] = plus - up
        change[9 + 4 * k] = minus + down
        change[10 + 4 * k] = minus - down
    return [f[index] - change[index] for index in range(19)]


def kernel(sizes, pop, sol, rates_in, out, held, relaxed, flag, blocked, xs, xr, ys, yr, es, er,
           osend, iflag, rates, own_sem, in_send, in_recv, x_send, x_recv, y_send, y_recv, e_send, e_recv,
           o_send, o_recv):
    gxn, gyn, gzn, nx, ny = sizes
    pair = gzn == 2
    gx, gy, gz = lax.axis_index("gx"), lax.axis_index("gy"), lax.axis_index("gz")
    row_block = gy * gzn + gz

    def device(dx, dy):
        block = lax.rem(row_block + dy + gyn * gzn, gyn * gzn)
        return (lax.rem(gx + dx + gxn, gxn), block // gzn, lax.rem(block, gzn))

    order = [0, nx - 1] + list(range(1, nx - 1))
    local = []
    rates_copy = pltpu.make_async_copy(rates_in, rates, own_sem.at[nx + 1])
    rates_copy.start()
    if pair:
        other = (gx, gy, 1 - gz)
        mine = pl.ds(pl.multiple_of(gz * ny, ny), ny)
        others = pl.ds(pl.multiple_of((1 - gz) * ny, ny), ny)
        for x in order:
            local.append(pltpu.make_async_copy(
                pop.at[:, x, mine, :], held.at[:, x, gz], own_sem.at[x]))
        local.append(pltpu.make_async_copy(sol.at[:, mine, :], iflag.at[:, gz], own_sem.at[nx]))
    else:
        for x in order:
            local.append(pltpu.make_async_copy(pop.at[:, x], held.at[:, x], own_sem.at[x]))
        local.append(pltpu.make_async_copy(sol, iflag, own_sem.at[nx]))
    for copy in local:
        copy.start()

    barrier = pltpu.get_barrier_semaphore()
    around = [(dx, dy) for dx in (-1, 0, 1) for dy in (-1, 0, 1) if (dx, dy) != (0, 0)]
    for dx, dy in around:
        pl.semaphore_signal(barrier, inc=1, device_id=device(dx, dy), device_id_type=MESH)
    pl.semaphore_wait(barrier, len(around))

    def remote(src, dst, send, recv, to):
        copy = pltpu.make_async_remote_copy(
            src_ref=src, dst_ref=dst, send_sem=send, recv_sem=recv,
            device_id=to, device_id_type=MESH)
        copy.start()
        return copy

    moved = []
    if pair:
        for x in order:
            moved.append(remote(pop.at[:, x, others, :], held.at[:, x, gz],
                                in_send.at[x], in_recv.at[x], other))
        moved.append(remote(sol.at[:, others, :], iflag.at[:, gz],
                            in_send.at[nx], in_recv.at[nx], other))

    shape = (gzn, ny, 128)
    row = lax.broadcasted_iota(jnp.int32, shape, 1)
    lane = lax.broadcasted_iota(jnp.int32, shape, 2)
    rates_copy.wait()
    rate = [rates[index] for index in range(19)]
    sent = list(moved)

    def arrived(index):
        local[index].wait()
        if pair:
            moved[index].wait_recv()

    def shifted(plane, halo, velocity):
        cx, cy, cz = velocity
        value = plane()
        if cy:
            value = jnp.where(row == (0 if cy > 0 else ny - 1),
                              jnp.broadcast_to(halo(), shape), pltpu.roll(value, cy % ny, 1))
        if cz:
            turned = pltpu.roll(value, cz % 128, 2)
            if cz > 0:
                swapped = jnp.concatenate([turned[-1:], turned[:-1]], axis=0)
            else:
                swapped = jnp.concatenate([turned[1:], turned[:1]], axis=0)
            value = jnp.where(lane == (0 if cz > 0 else 127), swapped, turned)
        return value

    def source(t, p, x, is_flag):
        cx, cy, cz = VELOCITY[p]
        sx = x - cx
        outside = sx < 0 or sx >= nx
        xd, yd = (0 if cx > 0 else 1), (0 if cy > 0 else 1)

        def plane():
            if outside:
                return xr[t, xd, 5 if is_flag else X_OUT[xd].index(p)]
            return flag[sx] if is_flag else relaxed[p, sx]

        def halo():
            if outside:
                return er[t, EDGE.index(p), 1 if is_flag else 0]
            return yr[t, yd, 5 if is_flag else Y_OUT[yd].index(p), sx]

        return shifted(plane, halo, (cx, cy, cz))

    for t in range(STEPS):
        last = t == STEPS - 1
        if t == 0:
            arrived(nx)
            for x in range(nx):
                flag[x] = iflag[x].astype(jnp.float32)
                for d, at in ((0, ny - 1), (1, 0)):
                    ys[0, d, 5, x] = flag[x, :, at : at + 1, :]
            xs[0, 0, 5] = flag[nx - 1]
            xs[0, 1, 5] = flag[0]
            for e, p in enumerate(EDGE):
                cx, cy, _ = VELOCITY[p]
                at = ny - 1 if cy > 0 else 0
                es[0, e, 1] = flag[nx - 1 if cx > 0 else 0, :, at : at + 1, :]
        count = 6 if t == 0 else 5
        ecount = 2 if t == 0 else 1
        x_copies, e_copies, y_copies = [], [], []
        for place, x in enumerate(order):
            if t == 0:
                arrived(place)
            values = collide([held[index, x] for index in range(19)], rate)
            for index in range(19):
                relaxed[index, x] = values[index]
            for d, at in ((0, ny - 1), (1, 0)):
                for k, p in enumerate(Y_OUT[d]):
                    ys[t, d, k, x] = values[p][:, at : at + 1, :]
            d = {nx - 1: 0, 0: 1}.get(x)
            if d is not None:
                for e, p in enumerate(EDGE):
                    cx, cy, _ = VELOCITY[p]
                    if (cx > 0) == (d == 0):
                        at = ny - 1 if cy > 0 else 0
                        es[t, e, 0] = values[p][:, at : at + 1, :]
                        e_copies.append(remote(
                            es.at[t, e, pl.ds(0, ecount)], er.at[t, e, pl.ds(0, ecount)],
                            e_send.at[t, e], e_recv.at[t, e], device(cx, cy)))
                for k, p in enumerate(X_OUT[d]):
                    xs[t, d, k] = values[p]
            if place == 1:
                wrap = jnp.where(gx == 0, 1, 0)
                for far in (wrap, 1 - wrap):
                    x_copies.append(remote(
                        xs.at[t, far, pl.ds(0, count)], xr.at[t, far, pl.ds(0, count)],
                        x_send.at[t, far], x_recv.at[t, far], device(1 - 2 * far, 0)))
        for d in (0, 1):
            y_copies.append(remote(
                ys.at[t, d, pl.ds(0, count)], yr.at[t, d, pl.ds(0, count)],
                y_send.at[t, d], y_recv.at[t, d], device(0, 1 if d == 0 else -1)))
        sent += x_copies + e_copies + y_copies
        for copy in y_copies:
            copy.wait_recv()
        for place, x in enumerate(order[2:] + order[:2]):
            if place == nx - 2:
                for copy in x_copies + e_copies:
                    copy.wait_recv()
            rock = flag[x] > 0.5
            for p in range(19):
                if p == 0:
                    value = relaxed[0, x]
                else:
                    if t == 0:
                        wall = source(0, p, x, True)
                        blocked[p, x] = wall
                    else:
                        wall = blocked[p, x]
                    value = jnp.where(wall > 0.5, relaxed[OPPOSITE[p], x], source(t, p, x, False))
                value = jnp.where(rock, 0.0, value)
                if not last:
                    held[p, x] = value
                elif pair:
                    first = gz == 0
                    out[p, x, mine, :] = jnp.where(first, value[0], value[1])
                    osend[p, x] = jnp.where(first, value[1], value[0])
                else:
                    out[p, x] = value
            if last and pair:
                copy = remote(osend.at[:, x], out.at[:, x, mine, :],
                              o_send.at[x], o_recv.at[x], other)
                sent.append(copy)
                moved.append(copy)
    if pair:
        for copy in moved[nx + 1:]:
            copy.wait_recv()
    for copy in sent:
        copy.wait_send()


def shards(sizes, populations, solid, rates):
    gxn, gyn, gzn, nx, ny = sizes
    pair = gzn == 2
    if not pair:
        populations = lax.all_to_all(
            populations.reshape(19, nx, gzn, ny, 128), "gz", 2, 2, tiled=True)
        solid = lax.all_to_all(solid.reshape(nx, gzn, ny, 128), "gz", 1, 1, tiled=True)
    f32, dma, vmem = jnp.float32, pltpu.SemaphoreType.DMA, pltpu.VMEM
    block = (gzn, ny, 128)
    line = (gzn, 1, 128)
    out = pl.pallas_call(
        functools.partial(kernel, sizes),
        out_shape=jax.ShapeDtypeStruct(populations.shape, f32),
        in_specs=[
            pl.BlockSpec(memory_space=pltpu.HBM),
            pl.BlockSpec(memory_space=pltpu.HBM),
            pl.BlockSpec(memory_space=pltpu.HBM),
        ],
        out_specs=pl.BlockSpec(memory_space=pltpu.VMEM),
        scratch_shapes=[
            vmem((19, nx) + block, f32),
            vmem((19, nx) + block, f32),
            vmem((nx,) + block, f32),
            vmem((19, nx) + block, f32),
            vmem((STEPS, 2, 6) + block, f32),
            vmem((STEPS, 2, 6) + block, f32),
            vmem((STEPS, 2, 6, nx) + line, f32),
            vmem((STEPS, 2, 6, nx) + line, f32),
            vmem((STEPS, 4, 2) + line, f32),
            vmem((STEPS, 4, 2) + line, f32),
            vmem((19, nx, ny, 128), f32),
            vmem((nx,) + block, jnp.int32),
            pltpu.SMEM((19,), f32),
            dma((nx + 2,)),
            dma((nx + 1,)),
            dma((nx + 1,)),
            dma((STEPS, 2)),
            dma((STEPS, 2)),
            dma((STEPS, 2)),
            dma((STEPS, 2)),
            dma((STEPS, 4)),
            dma((STEPS, 4)),
            dma((nx,)),
            dma((nx,)),
        ],
        compiler_params=pltpu.CompilerParams(
            collective_id=0, has_side_effects=True, vmem_limit_bytes=32 * 1024 * 1024),
    )(populations, solid, rates)
    if not pair:
        out = lax.all_to_all(out, "gz", 2, 2, tiled=True).reshape(19, nx, gzn * ny, 128)
    return out


def solution(mesh):
    gxn, gyn, gzn = mesh.shape["gx"], mesh.shape["gy"], mesh.shape["gz"]

    def run(populations, solid, rates):
        sizes = (gxn, gyn, gzn, populations.shape[1] // gxn, populations.shape[2] // (gyn * gzn))
        in_specs = (P(None, "gx", "gy", "gz"), P("gx", "gy", "gz"), P())
        out_specs = P(None, "gx", "gy", "gz")
        return jax.shard_map(functools.partial(shards, sizes), mesh=mesh, in_specs=in_specs,
                             out_specs=out_specs, check_vma=False)(populations, solid, rates)

    return run
```

```python
import functools

import jax
import jax.numpy as jnp
from jax import lax
from jax.experimental import pallas as pl
from jax.experimental.pallas import tpu as pltpu
from jax.sharding import PartitionSpec as P

STEPS = 3
VELOCITY = [
    (0, 0, 0), (1, 0, 0), (-1, 0, 0), (0, 1, 0), (0, -1, 0), (0, 0, 1), (0, 0, -1),
    (1, 1, 0), (-1, -1, 0), (1, -1, 0), (-1, 1, 0),
    (1, 0, 1), (-1, 0, -1), (1, 0, -1), (-1, 0, 1),
    (0, 1, 1), (0, -1, -1), (0, 1, -1), (0, -1, 1),
]
OPPOSITE = [0, 2, 1, 4, 3, 6, 5, 8, 7, 10, 9, 12, 11, 14, 13, 16, 15, 18, 17]
X_OUT = ([1, 7, 9, 11, 13], [2, 8, 10, 12, 14])
Y_OUT = ([3, 7, 10, 15, 17], [4, 8, 9, 16, 18])
EDGE = [7, 8, 9, 10]
MESH = pl.DeviceIdType.MESH


def collide(f, rate):
    pairs = [(index, index + 1) for index in range(1, 19, 2)]
    total = [f[a] + f[b] for a, b in pairs]
    diff = [f[a] - f[b] for a, b in pairs]
    density = f[0] + ((total[0] + total[1] + total[2]) + (total[3] + total[4])
                      + (total[5] + total[6]) + (total[7] + total[8]))
    jx = diff[0] + (diff[3] + diff[4]) + (diff[5] + diff[6])
    jy = diff[1] + (diff[3] - diff[4]) + (diff[7] + diff[8])
    jz = diff[2] + (diff[5] - diff[6]) + (diff[7] - diff[8])
    base = density - 1.5 * (jx * jx + jy * jy + jz * jz)
    projected = [jx, jy, jz, jx + jy, jx - jy, jx + jz, jx - jz, jy + jz, jy - jz]
    rest = f[0] - (1.0 / 3.0) * base
    even, odd = [], []
    for k in range(9):
        weight = 1.0 / 18.0 if k < 3 else 1.0 / 36.0
        p = projected[k]
        even.append(total[k] - (2.0 * weight) * (base + 4.5 * (p * p)))
        odd.append(diff[k] - (6.0 * weight) * p)
    xxyy, xxzz, yyzz = even[3] + even[4], even[5] + even[6], even[7] + even[8]
    xyy, xzz, yzz = odd[3] + odd[4], odd[5] + odd[6], odd[7] + odd[8]
    xxy, xxz, yyz = odd[3] - odd[4], odd[5] - odd[6], odd[7] - odd[8]
    one = rate[0] * (rest + ((even[0] + even[1] + even[2]) + (xxyy + xxzz + yyzz)))
    mx = rate[1] * (odd[0] + xyy + xzz)
    my = rate[2] * (odd[1] + xxy + yzz)
    mz = rate[3] * (odd[2] + xxz + yyz)
    xx = rate[4] * (even[0] + xxyy + xxzz)
    yy = rate[5] * (even[1] + xxyy + yyzz)
    zz = rate[6] * (even[2] + xxzz + yyzz)
    xy = rate[7] * (even[3] - even[4])
    xz = rate[8] * (even[5] - even[6])
    yz = rate[9] * (even[7] - even[8])
    xxy, xxz, xyy = rate[10] * xxy, rate[11] * xxz, rate[12] * xyy
    yyz, xzz, yzz = rate[13] * yyz, rate[14] * xzz, rate[15] * yzz
    xxyy, xxzz, yyzz = rate[16] * xxyy, rate[17] * xxzz, rate[18] * yyzz
    change = [None] * 19
    change[0] = one - (xx + yy + zz) + (xxyy + xxzz + yyzz)
    sums = [xx - xxyy - xxzz, yy - xxyy - yyzz, zz - xxzz - yyzz]
    diffs = [mx - xyy - xzz, my - xxy - yzz, mz - xxz - yyz]
    for k in range(3):
        change[1 + 2 * k] = 0.5 * (sums[k] + diffs[k])
        change[2 + 2 * k] = 0.5 * (sums[k] - diffs[k])
    for k, (s, d, a, b) in enumerate(
        [(xxyy, xy, xyy, xxy), (xxzz, xz, xzz, xxz), (yyzz, yz, yzz, yyz)]
    ):
        plus, minus = 0.25 * (s + d), 0.25 * (s - d)
        up, down = 0.25 * (a + b), 0.25 * (a - b)
        change[7 + 4 * k] = plus + up
        change[8 + 4 * k] = plus - up
        change[9 + 4 * k] = minus + down
        change[10 + 4 * k] = minus - down
    return [f[index] - change[index] for index in range(19)]


def kernel(sizes, pop, sol, rates_in, out, held, relaxed, flag, blocked, xs, xr, ys, yr, es, er,
           osend, iflag, rates, raw, iraw, fsend, xs0, ys0, es0, x0_send, x0_recv, y0_send, y0_recv,
           e0_send, e0_recv, own_sem, in_send, in_recv, x_send, x_recv, y_send, y_recv, e_send, e_recv,
           o_send, o_recv):
    gxn, gyn, gzn, nx, ny = sizes
    pair = gzn == 2
    gx, gy, gz = lax.axis_index("gx"), lax.axis_index("gy"), lax.axis_index("gz")
    row_block = gy * gzn + gz

    def device(dx, dy):
        block = lax.rem(row_block + dy + gyn * gzn, gyn * gzn)
        return (lax.rem(gx + dx + gxn, gxn), block // gzn, lax.rem(block, gzn))

    order = [0, nx - 1] + list(range(1, nx - 1))
    local = []
    rates_copy = pltpu.make_async_copy(rates_in, rates, own_sem.at[nx + 1])
    rates_copy.start()
    if pair:
        other = (gx, gy, 1 - gz)
        mine = pl.ds(pl.multiple_of(gz * ny, ny), ny)
        for x in order:
            local.append(pltpu.make_async_copy(pop.at[:, x], raw.at[:, x], own_sem.at[x]))
        local.append(pltpu.make_async_copy(sol, iraw, own_sem.at[nx]))
    else:
        for x in order:
            local.append(pltpu.make_async_copy(pop.at[:, x], held.at[:, x], own_sem.at[x]))
        local.append(pltpu.make_async_copy(sol, iflag, own_sem.at[nx]))
    for copy in local:
        copy.start()

    barrier = pltpu.get_barrier_semaphore()
    near, ahead, back = lax.rem(gx + 1, gxn), lax.rem(gy + 1, gyn), lax.rem(gy + gyn - 1, gyn)
    below = lax.rem(gx + gxn - 1, gxn)
    if pair:
        side = jnp.where(gz == 0, back, ahead)
        around = [other] + [(i, gy, k) for i in (below, near) for k in (0, 1)]
        around += [(i, side, k) for i in (below, gx, near) for k in (0, 1)]
    else:
        around = [device(dx, dy) for dx in (-1, 0, 1) for dy in (-1, 0, 1) if (dx, dy) != (0, 0)]
    for to in around:
        pl.semaphore_signal(barrier, inc=1, device_id=to, device_id_type=MESH)
    if not pair:
        pl.semaphore_wait(barrier, len(around))

    def remote(src, dst, send, recv, to):
        copy = pltpu.make_async_remote_copy(
            src_ref=src, dst_ref=dst, send_sem=send, recv_sem=recv,
            device_id=to, device_id_type=MESH)
        copy.start()
        return copy

    moved = []
    shape = (gzn, ny, 128)
    row = lax.broadcasted_iota(jnp.int32, shape, 1)
    lane = lax.broadcasted_iota(jnp.int32, shape, 2)
    rates_copy.wait()
    rate = [rates[index] for index in range(19)]
    sent = list(moved)

    def arrived(index):
        local[index].wait()

    def shifted(plane, halo, velocity):
        cx, cy, cz = velocity
        value = plane()
        if cy:
            value = jnp.where(row == (0 if cy > 0 else ny - 1),
                              jnp.broadcast_to(halo(), shape), pltpu.roll(value, cy % ny, 1))
        if cz:
            turned = pltpu.roll(value, cz % 128, 2)
            if cz > 0:
                swapped = jnp.concatenate([turned[-1:], turned[:-1]], axis=0)
            else:
                swapped = jnp.concatenate([turned[1:], turned[:1]], axis=0)
            value = jnp.where(lane == (0 if cz > 0 else 127), swapped, turned)
        return value

    def source(t, p, x, is_flag):
        cx, cy, cz = VELOCITY[p]
        sx = x - cx
        outside = sx < 0 or sx >= nx
        xd, yd = (0 if cx > 0 else 1), (0 if cy > 0 else 1)

        def plane():
            if outside:
                return xr[t, xd, 5 if is_flag else X_OUT[xd].index(p)]
            return flag[sx] if is_flag else relaxed[p, sx]

        def halo():
            if outside:
                return er[t, EDGE.index(p), 1 if is_flag else 0]
            return yr[t, yd, 5 if is_flag else Y_OUT[yd].index(p), sx]

        return shifted(plane, halo, (cx, cy, cz))

    def first_step():
        lower = gz == 0
        local[nx].wait()
        flags = [iraw[x].astype(jnp.float32) for x in range(nx)]
        part = lambda value, h: value[h * ny : (h + 1) * ny]
        line = lambda value, at: value[at : at + 1]
        feed = {(0, 1): ny - 1, (0, 0): 2 * ny - 1, (1, 0): ny, (1, 1): 0}

        def put_y(k, x, d, value):
            ys0[0, d, k, x] = line(value, feed[d, d])
            ys0[1, d, k, x] = line(value, feed[d, 1 - d])

        for x in range(nx):
            flag[x, gz] = jnp.where(lower, part(flags[x], 0), part(flags[x], 1))
            fsend[x] = jnp.where(lower, part(flags[x], 1), part(flags[x], 0))
            for d in (0, 1):
                put_y(5, x, d, flags[x])
        for h in (0, 1):
            xs0[h, 0, 5] = part(flags[nx - 1], h)
            xs0[h, 1, 5] = part(flags[0], h)
            for e, p in enumerate(EDGE):
                cx, cy, _ = VELOCITY[p]
                es0[h, e, 1] = line(flags[nx - 1 if cx > 0 else 0], feed[0 if cy > 0 else 1, h])

        def one(place, x):
            arrived(place)
            values = collide([raw[index, x] for index in range(19)], rate)
            for index in range(19):
                low, high = part(values[index], 0), part(values[index], 1)
                relaxed[index, x, gz] = jnp.where(lower, low, high)
                osend[index, x] = jnp.where(lower, high, low)
            for d in (0, 1):
                for k, p in enumerate(Y_OUT[d]):
                    put_y(k, x, d, values[p])
            return values

        faces = {x: one(place, x) for place, x in enumerate(order[:2])}
        for h in (0, 1):
            for e, p in enumerate(EDGE):
                cx, cy, _ = VELOCITY[p]
                es0[h, e, 0] = line(faces[nx - 1 if cx > 0 else 0][p], feed[0 if cy > 0 else 1, h])
            for k in range(5):
                xs0[h, 0, k] = part(faces[nx - 1][X_OUT[0][k]], h)
                xs0[h, 1, k] = part(faces[0][X_OUT[1][k]], h)
        pl.semaphore_wait(barrier, len(around))
        e_copies, x_copies, y_copies, r_copies = [], [], [], []
        for h in (0, 1):
            for e, p in enumerate(EDGE):
                cx, cy, _ = VELOCITY[p]
                to_y = gy if (cy > 0) == (h == 1) else (ahead if cy > 0 else back)
                e_copies.append(remote(es0.at[h, e], er.at[0, e, :, gz], e0_send.at[h, e],
                                       e0_recv.at[gz, e], (near if cx > 0 else below, to_y, h)))
        wrap = jnp.where(gx == 0, 1, 0)
        for far in (wrap, 1 - wrap):
            for h in (0, 1):
                x_copies.append(remote(
                    xs0.at[h, far], xr.at[0, far, :, gz], x0_send.at[h, far],
                    x0_recv.at[gz, far], (jnp.where(far == 0, near, below), gy, h)))
        for place, x in enumerate(order[2:]):
            one(place + 2, x)
        for d, to in ((0, (gx, ahead, 0)), (1, (gx, back, 1))):
            y_copies.append(remote(ys0.at[0, d], yr.at[0, d, :, :, gz], y0_send.at[d],
                                   y0_recv.at[gz], to))
        y_copies.append(remote(ys0.at[1, gz], yr.at[0, gz, :, :, gz], y0_send.at[2],
                               y0_recv.at[2], other))
        yr[0, 1 - gz, :, :, gz] = ys0[1, 1 - gz]
        r_copies.append(remote(fsend, flag.at[:, gz], in_send.at[nx], in_recv.at[nx], other))
        for x in order:
            r_copies.append(remote(osend.at[:, x], relaxed.at[:, x, gz], in_send.at[x],
                                   in_recv.at[x], other))

        def faces_in():
            for d in (0, 1):
                for k in (0, 1):
                    pltpu.make_async_remote_copy(
                        src_ref=xs0.at[k, d], dst_ref=xr.at[0, d, :, k], send_sem=x0_send.at[k, d],
                        recv_sem=x0_recv.at[k, d], device_id=other,
                        device_id_type=MESH).wait_recv()
            for e in range(4):
                for k in (0, 1):
                    pltpu.make_async_remote_copy(
                        src_ref=es0.at[k, e], dst_ref=er.at[0, e, :, k], send_sem=e0_send.at[k, e],
                        recv_sem=e0_recv.at[k, e], device_id=other,
                        device_id_type=MESH).wait_recv()

        def rows_in():
            for k in (0, 1):
                pltpu.make_async_remote_copy(
                    src_ref=ys0.at[0, 0], dst_ref=yr.at[0, gz, :, :, k], send_sem=y0_send.at[0],
                    recv_sem=y0_recv.at[k], device_id=other, device_id_type=MESH).wait_recv()
            pltpu.make_async_remote_copy(
                src_ref=ys0.at[1, gz], dst_ref=yr.at[0, 1 - gz, :, :, 1 - gz],
                send_sem=y0_send.at[2], recv_sem=y0_recv.at[2], device_id=other,
                device_id_type=MESH).wait_recv()
            for place, x in enumerate([nx] + order):
                pltpu.make_async_remote_copy(
                    src_ref=fsend if place == 0 else osend.at[:, x],
                    dst_ref=flag.at[:, 1 - gz] if place == 0 else relaxed.at[:, x, 1 - gz],
                    send_sem=in_send.at[x], recv_sem=in_recv.at[x], device_id=other,
                    device_id_type=MESH).wait_recv()

        for copy in r_copies:
            first_sends.append(copy)
        sent.extend(e_copies + x_copies + y_copies)
        return rows_in, faces_in

    first_sends = []
    rows_in = faces_in = None
    if pair:
        rows_in, faces_in = first_step()
    for t in range(STEPS):
        last = t == STEPS - 1
        if t == 0 and not pair:
            arrived(nx)
            for x in range(nx):
                flag[x] = iflag[x].astype(jnp.float32)
                for d, at in ((0, ny - 1), (1, 0)):
                    ys[0, d, 5, x] = flag[x, :, at : at + 1, :]
            xs[0, 0, 5] = flag[nx - 1]
            xs[0, 1, 5] = flag[0]
            for e, p in enumerate(EDGE):
                cx, cy, _ = VELOCITY[p]
                at = ny - 1 if cy > 0 else 0
                es[0, e, 1] = flag[nx - 1 if cx > 0 else 0, :, at : at + 1, :]
        count = 6 if t == 0 else 5
        ecount = 2 if t == 0 else 1
        x_copies, e_copies, y_copies = [], [], []
        for place, x in enumerate(order if t or not pair else []):
            if t == 0:
                arrived(place)
            values = collide([held[index, x] for index in range(19)], rate)
            for index in range(19):
                relaxed[index, x] = values[index]
            for d, at in ((0, ny - 1), (1, 0)):
                for k, p in enumerate(Y_OUT[d]):
                    ys[t, d, k, x] = values[p][:, at : at + 1, :]
            d = {nx - 1: 0, 0: 1}.get(x)
            if d is not None:
                for e, p in enumerate(EDGE):
                    cx, cy, _ = VELOCITY[p]
                    if (cx > 0) == (d == 0):
                        at = ny - 1 if cy > 0 else 0
                        es[t, e, 0] = values[p][:, at : at + 1, :]
                        e_copies.append(remote(
                            es.at[t, e, pl.ds(0, ecount)], er.at[t, e, pl.ds(0, ecount)],
                            e_send.at[t, e], e_recv.at[t, e], device(cx, cy)))
                for k, p in enumerate(X_OUT[d]):
                    xs[t, d, k] = values[p]
            if place == 1:
                wrap = jnp.where(gx == 0, 1, 0)
                for far in (wrap, 1 - wrap):
                    x_copies.append(remote(
                        xs.at[t, far, pl.ds(0, count)], xr.at[t, far, pl.ds(0, count)],
                        x_send.at[t, far], x_recv.at[t, far], device(1 - 2 * far, 0)))
        for d in (0, 1) if t or not pair else ():
            y_copies.append(remote(
                ys.at[t, d, pl.ds(0, count)], yr.at[t, d, pl.ds(0, count)],
                y_send.at[t, d], y_recv.at[t, d], device(0, 1 if d == 0 else -1)))
        sent += x_copies + e_copies + y_copies
        for copy in y_copies:
            copy.wait_recv()
        if t == 0 and pair:
            rows_in()
        for place, x in enumerate(order[2:] + order[:2]):
            if place == nx - 2:
                for copy in x_copies + e_copies:
                    copy.wait_recv()
                if t == 0 and pair:
                    faces_in()
            if last and place == 0:
                for copy in first_sends:
                    copy.wait_send()
            rock = flag[x] > 0.5
            for p in range(19):
                if p == 0:
                    value = relaxed[0, x]
                else:
                    if t == 0:
                        wall = source(0, p, x, True)
                        blocked[p, x] = wall
                    else:
                        wall = blocked[p, x]
                    value = jnp.where(wall > 0.5, relaxed[OPPOSITE[p], x], source(t, p, x, False))
                value = jnp.where(rock, 0.0, value)
                if not last:
                    held[p, x] = value
                elif pair:
                    first = gz == 0
                    out[p, x, mine, :] = jnp.where(first, value[0], value[1])
                    osend[p, x] = jnp.where(first, value[1], value[0])
                else:
                    out[p, x] = value
            if last and pair:
                copy = remote(osend.at[:, x], out.at[:, x, mine, :],
                              o_send.at[x], o_recv.at[x], other)
                sent.append(copy)
                moved.append(copy)
    if pair:
        for copy in moved:
            copy.wait_recv()
    for copy in sent:
        copy.wait_send()


def shards(sizes, populations, solid, rates):
    gxn, gyn, gzn, nx, ny = sizes
    pair = gzn == 2
    if not pair:
        populations = lax.all_to_all(
            populations.reshape(19, nx, gzn, ny, 128), "gz", 2, 2, tiled=True)
        solid = lax.all_to_all(solid.reshape(nx, gzn, ny, 128), "gz", 1, 1, tiled=True)
    f32, dma, vmem = jnp.float32, pltpu.SemaphoreType.DMA, pltpu.VMEM
    block = (gzn, ny, 128)
    line = (gzn, 1, 128)
    out = pl.pallas_call(
        functools.partial(kernel, sizes),
        out_shape=jax.ShapeDtypeStruct(populations.shape, f32),
        in_specs=[
            pl.BlockSpec(memory_space=pltpu.HBM),
            pl.BlockSpec(memory_space=pltpu.HBM),
            pl.BlockSpec(memory_space=pltpu.HBM),
        ],
        out_specs=pl.BlockSpec(memory_space=pltpu.VMEM),
        scratch_shapes=[
            vmem((19, nx) + block, f32),
            vmem((19, nx) + block, f32),
            vmem((nx,) + block, f32),
            vmem((19, nx) + block, f32),
            vmem((STEPS, 2, 6) + block, f32),
            vmem((STEPS, 2, 6) + block, f32),
            vmem((STEPS, 2, 6, nx) + line, f32),
            vmem((STEPS, 2, 6, nx) + line, f32),
            vmem((STEPS, 4, 2) + line, f32),
            vmem((STEPS, 4, 2) + line, f32),
            vmem((19, nx, ny, 128), f32),
            vmem((nx,) + block, jnp.int32),
            pltpu.SMEM((19,), f32),
            vmem((19, nx, gzn * ny, 128), f32),
            vmem((nx, gzn * ny, 128), jnp.int32),
            vmem((nx, ny, 128), f32),
            vmem((2, 2, 6, ny, 128), f32),
            vmem((2, 2, 6, nx, 1, 128), f32),
            vmem((2, 4, 2, 1, 128), f32),
            dma((2, 2)),
            dma((2, 2)),
            dma((3,)),
            dma((3,)),
            dma((2, 4)),
            dma((2, 4)),
            dma((nx + 2,)),
            dma((nx + 1,)),
            dma((nx + 1,)),
            dma((STEPS, 2)),
            dma((STEPS, 2)),
            dma((STEPS, 2)),
            dma((STEPS, 2)),
            dma((STEPS, 4)),
            dma((STEPS, 4)),
            dma((nx,)),
            dma((nx,)),
        ],
        compiler_params=pltpu.CompilerParams(
            collective_id=0, has_side_effects=True, vmem_limit_bytes=32 * 1024 * 1024),
    )(populations, solid, rates)
    if not pair:
        out = lax.all_to_all(out, "gz", 2, 2, tiled=True).reshape(19, nx, gzn * ny, 128)
    return out


def solution(mesh):
    gxn, gyn, gzn = mesh.shape["gx"], mesh.shape["gy"], mesh.shape["gz"]

    def run(populations, solid, rates):
        sizes = (gxn, gyn, gzn, populations.shape[1] // gxn, populations.shape[2] // (gyn * gzn))
        in_specs = (P(None, "gx", "gy", "gz"), P("gx", "gy", "gz"), P())
        out_specs = P(None, "gx", "gy", "gz")
        return jax.shard_map(functools.partial(shards, sizes), mesh=mesh, in_specs=in_specs,
                             out_specs=out_specs, check_vma=False)(populations, solid, rates)

    return run
```

```python
import functools

import jax
import jax.numpy as jnp
from jax import lax
from jax.experimental import pallas as pl
from jax.experimental.pallas import tpu as pltpu
from jax.sharding import PartitionSpec as P

STEPS = 3
VELOCITY = [
    (0, 0, 0), (1, 0, 0), (-1, 0, 0), (0, 1, 0), (0, -1, 0), (0, 0, 1), (0, 0, -1),
    (1, 1, 0), (-1, -1, 0), (1, -1, 0), (-1, 1, 0),
    (1, 0, 1), (-1, 0, -1), (1, 0, -1), (-1, 0, 1),
    (0, 1, 1), (0, -1, -1), (0, 1, -1), (0, -1, 1),
]
OPPOSITE = [0, 2, 1, 4, 3, 6, 5, 8, 7, 10, 9, 12, 11, 14, 13, 16, 15, 18, 17]
X_OUT = ([1, 7, 9, 11, 13], [2, 8, 10, 12, 14])
Y_OUT = ([3, 7, 10, 15, 17], [4, 8, 9, 16, 18])
EDGE = [7, 8, 9, 10]
MESH = pl.DeviceIdType.MESH


def collide(f, rate):
    pairs = [(index, index + 1) for index in range(1, 19, 2)]
    total = [f[a] + f[b] for a, b in pairs]
    diff = [f[a] - f[b] for a, b in pairs]
    density = f[0] + ((total[0] + total[1] + total[2]) + (total[3] + total[4])
                      + (total[5] + total[6]) + (total[7] + total[8]))
    jx = diff[0] + (diff[3] + diff[4]) + (diff[5] + diff[6])
    jy = diff[1] + (diff[3] - diff[4]) + (diff[7] + diff[8])
    jz = diff[2] + (diff[5] - diff[6]) + (diff[7] - diff[8])
    base = density - 1.5 * (jx * jx + jy * jy + jz * jz)
    projected = [jx, jy, jz, jx + jy, jx - jy, jx + jz, jx - jz, jy + jz, jy - jz]
    rest = f[0] - (1.0 / 3.0) * base
    even, odd = [], []
    for k in range(9):
        weight = 1.0 / 18.0 if k < 3 else 1.0 / 36.0
        p = projected[k]
        even.append(total[k] - (2.0 * weight) * (base + 4.5 * (p * p)))
        odd.append(diff[k] - (6.0 * weight) * p)
    xxyy, xxzz, yyzz = even[3] + even[4], even[5] + even[6], even[7] + even[8]
    xyy, xzz, yzz = odd[3] + odd[4], odd[5] + odd[6], odd[7] + odd[8]
    xxy, xxz, yyz = odd[3] - odd[4], odd[5] - odd[6], odd[7] - odd[8]
    one = rate[0] * (rest + ((even[0] + even[1] + even[2]) + (xxyy + xxzz + yyzz)))
    mx = rate[1] * (odd[0] + xyy + xzz)
    my = rate[2] * (odd[1] + xxy + yzz)
    mz = rate[3] * (odd[2] + xxz + yyz)
    xx = rate[4] * (even[0] + xxyy + xxzz)
    yy = rate[5] * (even[1] + xxyy + yyzz)
    zz = rate[6] * (even[2] + xxzz + yyzz)
    xy = rate[7] * (even[3] - even[4])
    xz = rate[8] * (even[5] - even[6])
    yz = rate[9] * (even[7] - even[8])
    xxy, xxz, xyy = rate[10] * xxy, rate[11] * xxz, rate[12] * xyy
    yyz, xzz, yzz = rate[13] * yyz, rate[14] * xzz, rate[15] * yzz
    xxyy, xxzz, yyzz = rate[16] * xxyy, rate[17] * xxzz, rate[18] * yyzz
    change = [None] * 19
    change[0] = one - (xx + yy + zz) + (xxyy + xxzz + yyzz)
    sums = [xx - xxyy - xxzz, yy - xxyy - yyzz, zz - xxzz - yyzz]
    diffs = [mx - xyy - xzz, my - xxy - yzz, mz - xxz - yyz]
    for k in range(3):
        change[1 + 2 * k] = 0.5 * (sums[k] + diffs[k])
        change[2 + 2 * k] = 0.5 * (sums[k] - diffs[k])
    for k, (s, d, a, b) in enumerate(
        [(xxyy, xy, xyy, xxy), (xxzz, xz, xzz, xxz), (yyzz, yz, yzz, yyz)]
    ):
        plus, minus = 0.25 * (s + d), 0.25 * (s - d)
        up, down = 0.25 * (a + b), 0.25 * (a - b)
        change[7 + 4 * k] = plus + up
        change[8 + 4 * k] = plus - up
        change[9 + 4 * k] = minus + down
        change[10 + 4 * k] = minus - down
    return [f[index] - change[index] for index in range(19)]


def kernel(sizes, pop, sol, rates_in, out, held, relaxed, flag, blocked, xs, xr, ys, yr, es, er,
           osend, iflag, rates, raw, iraw, fsend, xs0, ys0, es0, x0_send, x0_recv, y0_send, y0_recv,
           e0_send, e0_recv, own_sem, in_send, in_recv, x_send, x_recv, y_send, y_recv, e_send, e_recv,
           o_send, o_recv):
    gxn, gyn, gzn, nx, ny = sizes
    pair = gzn == 2
    gx, gy, gz = lax.axis_index("gx"), lax.axis_index("gy"), lax.axis_index("gz")
    row_block = gy * gzn + gz

    def device(dx, dy):
        block = lax.rem(row_block + dy + gyn * gzn, gyn * gzn)
        return (lax.rem(gx + dx + gxn, gxn), block // gzn, lax.rem(block, gzn))

    order = [0, nx - 1] + list(range(1, nx - 1))
    local = []
    rates_copy = pltpu.make_async_copy(rates_in, rates, own_sem.at[nx + 1])
    rates_copy.start()
    if pair:
        other = (gx, gy, 1 - gz)
        mine = pl.ds(pl.multiple_of(gz * ny, ny), ny)
        for x in order:
            local.append(pltpu.make_async_copy(pop.at[:, x], raw.at[:, x], own_sem.at[x]))
        local.append(pltpu.make_async_copy(sol, iraw, own_sem.at[nx]))
    else:
        for x in order:
            local.append(pltpu.make_async_copy(pop.at[:, x], held.at[:, x], own_sem.at[x]))
        local.append(pltpu.make_async_copy(sol, iflag, own_sem.at[nx]))

    barrier = pltpu.get_barrier_semaphore()
    near, ahead, back = lax.rem(gx + 1, gxn), lax.rem(gy + 1, gyn), lax.rem(gy + gyn - 1, gyn)
    below = lax.rem(gx + gxn - 1, gxn)
    if pair:
        side = jnp.where(gz == 0, back, ahead)
        around = [(i, side, k) for i in (below, near, gx) for k in (0, 1)]
        around += [(i, gy, k) for i in (below, near) for k in (0, 1)] + [other]
    else:
        around = [device(dx, dy) for dx in (-1, 0, 1) for dy in (-1, 0, 1) if (dx, dy) != (0, 0)]
    for to in around:
        pl.semaphore_signal(barrier, inc=1, device_id=to, device_id_type=MESH)
    for copy in local:
        copy.start()
    if not pair:
        pl.semaphore_wait(barrier, len(around))

    def remote(src, dst, send, recv, to):
        copy = pltpu.make_async_remote_copy(
            src_ref=src, dst_ref=dst, send_sem=send, recv_sem=recv,
            device_id=to, device_id_type=MESH)
        copy.start()
        return copy

    moved = []
    shape = (gzn, ny, 128)
    row = lax.broadcasted_iota(jnp.int32, shape, 1)
    lane = lax.broadcasted_iota(jnp.int32, shape, 2)
    rates_copy.wait()
    rate = [rates[index] for index in range(19)]
    sent = list(moved)
    leaving = []

    def arrived(index):
        local[index].wait()

    def shifted(plane, halo, velocity):
        cx, cy, cz = velocity
        value = plane()
        if cy:
            value = jnp.where(row == (0 if cy > 0 else ny - 1),
                              jnp.broadcast_to(halo(), shape), pltpu.roll(value, cy % ny, 1))
        if cz:
            turned = pltpu.roll(value, cz % 128, 2)
            if cz > 0:
                swapped = jnp.concatenate([turned[-1:], turned[:-1]], axis=0)
            else:
                swapped = jnp.concatenate([turned[1:], turned[:1]], axis=0)
            value = jnp.where(lane == (0 if cz > 0 else 127), swapped, turned)
        return value

    def source(t, p, x, is_flag):
        cx, cy, cz = VELOCITY[p]
        sx = x - cx
        outside = sx < 0 or sx >= nx
        xd, yd = (0 if cx > 0 else 1), (0 if cy > 0 else 1)

        def plane():
            if outside:
                return xr[t, xd, 5 if is_flag else X_OUT[xd].index(p)]
            return flag[sx] if is_flag else relaxed[p, sx]

        def halo():
            if outside:
                return er[t, EDGE.index(p), 1 if is_flag else 0]
            return yr[t, yd, 5 if is_flag else Y_OUT[yd].index(p), sx]

        return shifted(plane, halo, (cx, cy, cz))

    def first_step():
        lower = gz == 0
        local[nx].wait()
        flags = [iraw[x].astype(jnp.float32) for x in range(nx)]
        part = lambda value, h: value[h * ny : (h + 1) * ny]
        line = lambda value, at: value[at : at + 1]
        feed = {(0, 1): ny - 1, (0, 0): 2 * ny - 1, (1, 0): ny, (1, 1): 0}

        def put_y(k, x, d, value):
            ys0[0, d, k, x] = line(value, feed[d, d])
            ys0[1, d, k, x] = line(value, feed[d, 1 - d])

        for x in range(nx):
            flag[x, gz] = jnp.where(lower, part(flags[x], 0), part(flags[x], 1))
            fsend[x] = jnp.where(lower, part(flags[x], 1), part(flags[x], 0))
            for d in (0, 1):
                put_y(5, x, d, flags[x])
        for h in (0, 1):
            xs0[h, 0, 5] = part(flags[nx - 1], h)
            xs0[h, 1, 5] = part(flags[0], h)
            for e, p in enumerate(EDGE):
                cx, cy, _ = VELOCITY[p]
                es0[h, e, 1] = line(flags[nx - 1 if cx > 0 else 0], feed[0 if cy > 0 else 1, h])

        def one(place, x):
            arrived(place)
            values = collide([raw[index, x] for index in range(19)], rate)
            for index in range(19):
                low, high = part(values[index], 0), part(values[index], 1)
                relaxed[index, x, gz] = jnp.where(lower, low, high)
                osend[index, x] = jnp.where(lower, high, low)
            for d in (0, 1):
                for k, p in enumerate(Y_OUT[d]):
                    put_y(k, x, d, values[p])
            return values

        faces = {x: one(place, x) for place, x in enumerate(order[:2])}
        for h in (0, 1):
            for e, p in enumerate(EDGE):
                cx, cy, _ = VELOCITY[p]
                es0[h, e, 0] = line(faces[nx - 1 if cx > 0 else 0][p], feed[0 if cy > 0 else 1, h])
            for k in range(5):
                xs0[h, 0, k] = part(faces[nx - 1][X_OUT[0][k]], h)
                xs0[h, 1, k] = part(faces[0][X_OUT[1][k]], h)
        pl.semaphore_wait(barrier, len(around))
        e_copies, x_copies, y_copies, r_copies = [], [], [], []
        for h in (0, 1):
            for e, p in enumerate(EDGE):
                cx, cy, _ = VELOCITY[p]
                to_y = gy if (cy > 0) == (h == 1) else (ahead if cy > 0 else back)
                e_copies.append(remote(es0.at[h, e], er.at[0, e, :, gz], e0_send.at[h, e],
                                       e0_recv.at[gz, e], (near if cx > 0 else below, to_y, h)))
        wrap = jnp.where(gx == 0, 1, 0)
        for far in (wrap, 1 - wrap):
            for h in (0, 1):
                x_copies.append(remote(
                    xs0.at[h, far], xr.at[0, far, :, gz], x0_send.at[h, far],
                    x0_recv.at[gz, far], (jnp.where(far == 0, near, below), gy, h)))
        for place, x in enumerate(order[2:]):
            one(place + 2, x)
        for d, to in ((0, (gx, ahead, 0)), (1, (gx, back, 1))):
            y_copies.append(remote(ys0.at[0, d], yr.at[0, d, :, :, gz], y0_send.at[d],
                                   y0_recv.at[gz], to))
        y_copies.append(remote(ys0.at[1, gz], yr.at[0, gz, :, :, gz], y0_send.at[2],
                               y0_recv.at[2], other))
        yr[0, 1 - gz, :, :, gz] = ys0[1, 1 - gz]
        r_copies.append(remote(fsend, flag.at[:, gz], in_send.at[nx], in_recv.at[nx], other))
        for x in order:
            r_copies.append(remote(osend.at[:, x], relaxed.at[:, x, gz], in_send.at[x],
                                   in_recv.at[x], other))

        def faces_in():
            for d in (0, 1):
                for k in (0, 1):
                    pltpu.make_async_remote_copy(
                        src_ref=xs0.at[k, d], dst_ref=xr.at[0, d, :, k], send_sem=x0_send.at[k, d],
                        recv_sem=x0_recv.at[k, d], device_id=other,
                        device_id_type=MESH).wait_recv()
            for e in range(4):
                for k in (0, 1):
                    pltpu.make_async_remote_copy(
                        src_ref=es0.at[k, e], dst_ref=er.at[0, e, :, k], send_sem=e0_send.at[k, e],
                        recv_sem=e0_recv.at[k, e], device_id=other,
                        device_id_type=MESH).wait_recv()

        def rows_in():
            for k in (0, 1):
                pltpu.make_async_remote_copy(
                    src_ref=ys0.at[0, 0], dst_ref=yr.at[0, gz, :, :, k], send_sem=y0_send.at[0],
                    recv_sem=y0_recv.at[k], device_id=other, device_id_type=MESH).wait_recv()
            pltpu.make_async_remote_copy(
                src_ref=ys0.at[1, gz], dst_ref=yr.at[0, 1 - gz, :, :, 1 - gz],
                send_sem=y0_send.at[2], recv_sem=y0_recv.at[2], device_id=other,
                device_id_type=MESH).wait_recv()
            for place, x in enumerate([nx] + order):
                pltpu.make_async_remote_copy(
                    src_ref=fsend if place == 0 else osend.at[:, x],
                    dst_ref=flag.at[:, 1 - gz] if place == 0 else relaxed.at[:, x, 1 - gz],
                    send_sem=in_send.at[x], recv_sem=in_recv.at[x], device_id=other,
                    device_id_type=MESH).wait_recv()

        for copy in r_copies:
            first_sends.append(copy)
        sent.extend(e_copies + x_copies + y_copies)
        return rows_in, faces_in

    first_sends = []
    rows_in = faces_in = None
    if pair:
        rows_in, faces_in = first_step()
    for t in range(STEPS):
        last = t == STEPS - 1
        if t == 0 and not pair:
            arrived(nx)
            for x in range(nx):
                flag[x] = iflag[x].astype(jnp.float32)
                for d, at in ((0, ny - 1), (1, 0)):
                    ys[0, d, 5, x] = flag[x, :, at : at + 1, :]
            xs[0, 0, 5] = flag[nx - 1]
            xs[0, 1, 5] = flag[0]
            for e, p in enumerate(EDGE):
                cx, cy, _ = VELOCITY[p]
                at = ny - 1 if cy > 0 else 0
                es[0, e, 1] = flag[nx - 1 if cx > 0 else 0, :, at : at + 1, :]
        count = 6 if t == 0 else 5
        ecount = 2 if t == 0 else 1
        x_copies, e_copies, y_copies = [], [], []
        for place, x in enumerate(order if t or not pair else []):
            if t == 0:
                arrived(place)
            values = collide([held[index, x] for index in range(19)], rate)
            for index in range(19):
                relaxed[index, x] = values[index]
            for d, at in ((0, ny - 1), (1, 0)):
                for k, p in enumerate(Y_OUT[d]):
                    ys[t, d, k, x] = values[p][:, at : at + 1, :]
            d = {nx - 1: 0, 0: 1}.get(x)
            if d is not None:
                for e, p in enumerate(EDGE):
                    cx, cy, _ = VELOCITY[p]
                    if (cx > 0) == (d == 0):
                        at = ny - 1 if cy > 0 else 0
                        es[t, e, 0] = values[p][:, at : at + 1, :]
                        e_copies.append(remote(
                            es.at[t, e, pl.ds(0, ecount)], er.at[t, e, pl.ds(0, ecount)],
                            e_send.at[t, e], e_recv.at[t, e], device(cx, cy)))
                for k, p in enumerate(X_OUT[d]):
                    xs[t, d, k] = values[p]
            if place == 1:
                wrap = jnp.where(gx == 0, 1, 0)
                for far in (wrap, 1 - wrap):
                    x_copies.append(remote(
                        xs.at[t, far, pl.ds(0, count)], xr.at[t, far, pl.ds(0, count)],
                        x_send.at[t, far], x_recv.at[t, far], device(1 - 2 * far, 0)))
        for d in (0, 1) if t or not pair else ():
            y_copies.append(remote(
                ys.at[t, d, pl.ds(0, count)], yr.at[t, d, pl.ds(0, count)],
                y_send.at[t, d], y_recv.at[t, d], device(0, 1 if d == 0 else -1)))
        while sent:
            sent.pop().wait_send()
        sent += x_copies + e_copies + y_copies
        if last:
            while first_sends:
                first_sends.pop().wait_send()
        for copy in y_copies:
            copy.wait_recv()
        if t == 0 and pair:
            rows_in()
        for place, x in enumerate(order[2:] + order[:2]):
            if place == nx - 2:
                if last:
                    while sent and len(sent) > len(leaving):
                        sent.pop(0).wait_send()
                for copy in x_copies + e_copies:
                    copy.wait_recv()
                if t == 0 and pair:
                    faces_in()
            rock = flag[x] > 0.5
            for p in range(19):
                if p == 0:
                    value = relaxed[0, x]
                else:
                    if t == 0:
                        wall = source(0, p, x, True)
                        blocked[p, x] = wall
                    else:
                        wall = blocked[p, x]
                    value = jnp.where(wall > 0.5, relaxed[OPPOSITE[p], x], source(t, p, x, False))
                value = jnp.where(rock, 0.0, value)
                if not last:
                    held[p, x] = value
                elif pair:
                    first = gz == 0
                    out[p, x, mine, :] = jnp.where(first, value[0], value[1])
                    osend[p, x] = jnp.where(first, value[1], value[0])
                else:
                    out[p, x] = value
            if last and pair:
                copy = remote(osend.at[:, x], out.at[:, x, mine, :],
                              o_send.at[x], o_recv.at[x], other)
                sent.append(copy)
                leaving.append(copy)
                moved.append(copy)
    if pair:
        for copy in moved:
            copy.wait_recv()
    for copy in sent:
        copy.wait_send()


def shards(sizes, populations, solid, rates):
    gxn, gyn, gzn, nx, ny = sizes
    pair = gzn == 2
    if not pair:
        populations = lax.all_to_all(
            populations.reshape(19, nx, gzn, ny, 128), "gz", 2, 2, tiled=True)
        solid = lax.all_to_all(solid.reshape(nx, gzn, ny, 128), "gz", 1, 1, tiled=True)
    f32, dma, vmem = jnp.float32, pltpu.SemaphoreType.DMA, pltpu.VMEM
    block = (gzn, ny, 128)
    line = (gzn, 1, 128)
    out = pl.pallas_call(
        functools.partial(kernel, sizes),
        out_shape=jax.ShapeDtypeStruct(populations.shape, f32),
        in_specs=[
            pl.BlockSpec(memory_space=pltpu.HBM),
            pl.BlockSpec(memory_space=pltpu.HBM),
            pl.BlockSpec(memory_space=pltpu.HBM),
        ],
        out_specs=pl.BlockSpec(memory_space=pltpu.VMEM),
        scratch_shapes=[
            vmem((19, nx) + block, f32),
            vmem((19, nx) + block, f32),
            vmem((nx,) + block, f32),
            vmem((19, nx) + block, f32),
            vmem((STEPS, 2, 6) + block, f32),
            vmem((STEPS, 2, 6) + block, f32),
            vmem((STEPS, 2, 6, nx) + line, f32),
            vmem((STEPS, 2, 6, nx) + line, f32),
            vmem((STEPS, 4, 2) + line, f32),
            vmem((STEPS, 4, 2) + line, f32),
            vmem((19, nx, ny, 128), f32),
            vmem((nx,) + block, jnp.int32),
            pltpu.SMEM((19,), f32),
            vmem((19, nx, gzn * ny, 128), f32),
            vmem((nx, gzn * ny, 128), jnp.int32),
            vmem((nx, ny, 128), f32),
            vmem((2, 2, 6, ny, 128), f32),
            vmem((2, 2, 6, nx, 1, 128), f32),
            vmem((2, 4, 2, 1, 128), f32),
            dma((2, 2)),
            dma((2, 2)),
            dma((3,)),
            dma((3,)),
            dma((2, 4)),
            dma((2, 4)),
            dma((nx + 2,)),
            dma((nx + 1,)),
            dma((nx + 1,)),
            dma((STEPS, 2)),
            dma((STEPS, 2)),
            dma((STEPS, 2)),
            dma((STEPS, 2)),
            dma((STEPS, 4)),
            dma((STEPS, 4)),
            dma((nx,)),
            dma((nx,)),
        ],
        compiler_params=pltpu.CompilerParams(
            collective_id=0, has_side_effects=True, vmem_limit_bytes=32 * 1024 * 1024),
    )(populations, solid, rates)
    if not pair:
        out = lax.all_to_all(out, "gz", 2, 2, tiled=True).reshape(19, nx, gzn * ny, 128)
    return out


def solution(mesh):
    gxn, gyn, gzn = mesh.shape["gx"], mesh.shape["gy"], mesh.shape["gz"]

    def run(populations, solid, rates):
        sizes = (gxn, gyn, gzn, populations.shape[1] // gxn, populations.shape[2] // (gyn * gzn))
        in_specs = (P(None, "gx", "gy", "gz"), P("gx", "gy", "gz"), P())
        out_specs = P(None, "gx", "gy", "gz")
        return jax.shard_map(functools.partial(shards, sizes), mesh=mesh, in_specs=in_specs,
                             out_specs=out_specs, check_vma=False)(populations, solid, rates)

    return run
```

```python
import functools

import jax
import jax.numpy as jnp
from jax import lax
from jax.experimental import pallas as pl
from jax.experimental.pallas import tpu as pltpu
from jax.sharding import PartitionSpec as P

STEPS = 3
VELOCITY = [
    (0, 0, 0), (1, 0, 0), (-1, 0, 0), (0, 1, 0), (0, -1, 0), (0, 0, 1), (0, 0, -1),
    (1, 1, 0), (-1, -1, 0), (1, -1, 0), (-1, 1, 0),
    (1, 0, 1), (-1, 0, -1), (1, 0, -1), (-1, 0, 1),
    (0, 1, 1), (0, -1, -1), (0, 1, -1), (0, -1, 1),
]
OPPOSITE = [0, 2, 1, 4, 3, 6, 5, 8, 7, 10, 9, 12, 11, 14, 13, 16, 15, 18, 17]
X_OUT = ([1, 7, 9, 11, 13], [2, 8, 10, 12, 14])
Y_OUT = ([3, 7, 10, 15, 17], [4, 8, 9, 16, 18])
EDGE = [7, 8, 9, 10]
MESH = pl.DeviceIdType.MESH


def collide(f, rate):
    pairs = [(index, index + 1) for index in range(1, 19, 2)]
    total = [f[a] + f[b] for a, b in pairs]
    diff = [f[a] - f[b] for a, b in pairs]
    density = f[0] + ((total[0] + total[1] + total[2]) + (total[3] + total[4])
                      + (total[5] + total[6]) + (total[7] + total[8]))
    jx = diff[0] + (diff[3] + diff[4]) + (diff[5] + diff[6])
    jy = diff[1] + (diff[3] - diff[4]) + (diff[7] + diff[8])
    jz = diff[2] + (diff[5] - diff[6]) + (diff[7] - diff[8])
    base = density - 1.5 * (jx * jx + jy * jy + jz * jz)
    projected = [jx, jy, jz, jx + jy, jx - jy, jx + jz, jx - jz, jy + jz, jy - jz]
    rest = f[0] - (1.0 / 3.0) * base
    even, odd = [], []
    for k in range(9):
        weight = 1.0 / 18.0 if k < 3 else 1.0 / 36.0
        p = projected[k]
        even.append(total[k] - (2.0 * weight) * (base + 4.5 * (p * p)))
        odd.append(diff[k] - (6.0 * weight) * p)
    xxyy, xxzz, yyzz = even[3] + even[4], even[5] + even[6], even[7] + even[8]
    xyy, xzz, yzz = odd[3] + odd[4], odd[5] + odd[6], odd[7] + odd[8]
    xxy, xxz, yyz = odd[3] - odd[4], odd[5] - odd[6], odd[7] - odd[8]
    one = rate[0] * (rest + ((even[0] + even[1] + even[2]) + (xxyy + xxzz + yyzz)))
    mx = rate[1] * (odd[0] + xyy + xzz)
    my = rate[2] * (odd[1] + xxy + yzz)
    mz = rate[3] * (odd[2] + xxz + yyz)
    xx = rate[4] * (even[0] + xxyy + xxzz)
    yy = rate[5] * (even[1] + xxyy + yyzz)
    zz = rate[6] * (even[2] + xxzz + yyzz)
    xy = rate[7] * (even[3] - even[4])
    xz = rate[8] * (even[5] - even[6])
    yz = rate[9] * (even[7] - even[8])
    xxy, xxz, xyy = rate[10] * xxy, rate[11] * xxz, rate[12] * xyy
    yyz, xzz, yzz = rate[13] * yyz, rate[14] * xzz, rate[15] * yzz
    xxyy, xxzz, yyzz = rate[16] * xxyy, rate[17] * xxzz, rate[18] * yyzz
    change = [None] * 19
    change[0] = one - (xx + yy + zz) + (xxyy + xxzz + yyzz)
    sums = [xx - xxyy - xxzz, yy - xxyy - yyzz, zz - xxzz - yyzz]
    diffs = [mx - xyy - xzz, my - xxy - yzz, mz - xxz - yyz]
    for k in range(3):
        change[1 + 2 * k] = 0.5 * (sums[k] + diffs[k])
        change[2 + 2 * k] = 0.5 * (sums[k] - diffs[k])
    for k, (s, d, a, b) in enumerate(
        [(xxyy, xy, xyy, xxy), (xxzz, xz, xzz, xxz), (yyzz, yz, yzz, yyz)]
    ):
        plus, minus = 0.25 * (s + d), 0.25 * (s - d)
        up, down = 0.25 * (a + b), 0.25 * (a - b)
        change[7 + 4 * k] = plus + up
        change[8 + 4 * k] = plus - up
        change[9 + 4 * k] = minus + down
        change[10 + 4 * k] = minus - down
    return [f[index] - change[index] for index in range(19)]


def kernel(sizes, pop, sol, rates_in, out, held, relaxed, flag, blocked, xs, xr, ys, yr, es, er,
           osend, iflag, rates, raw, iraw, fsend, xs0, ys0, es0, x0_send, x0_recv, y0_send, y0_recv,
           e0_send, e0_recv, own_sem, in_send, in_recv, x_send, x_recv, y_send, y_recv, e_send, e_recv,
           o_send, o_recv):
    gxn, gyn, gzn, nx, ny = sizes
    pair = gzn == 2
    gx, gy, gz = lax.axis_index("gx"), lax.axis_index("gy"), lax.axis_index("gz")
    row_block = gy * gzn + gz

    def device(dx, dy):
        block = lax.rem(row_block + dy + gyn * gzn, gyn * gzn)
        return (lax.rem(gx + dx + gxn, gxn), block // gzn, lax.rem(block, gzn))

    order = [0, nx - 1] + list(range(1, nx - 1))
    local = []
    rates_copy = pltpu.make_async_copy(rates_in, rates, own_sem.at[nx + 1])
    rates_copy.start()
    if pair:
        other = (gx, gy, 1 - gz)
        mine = pl.ds(pl.multiple_of(gz * ny, ny), ny)
        for x in order:
            local.append(pltpu.make_async_copy(pop.at[:, x], raw.at[:, x], own_sem.at[x]))
        local.append(pltpu.make_async_copy(sol, iraw, own_sem.at[nx]))
    else:
        for x in order:
            local.append(pltpu.make_async_copy(pop.at[:, x], held.at[:, x], own_sem.at[x]))
        local.append(pltpu.make_async_copy(sol, iflag, own_sem.at[nx]))

    barrier = pltpu.get_barrier_semaphore()
    near, ahead, back = lax.rem(gx + 1, gxn), lax.rem(gy + 1, gyn), lax.rem(gy + gyn - 1, gyn)
    below = lax.rem(gx + gxn - 1, gxn)
    if pair:
        side = jnp.where(gz == 0, back, ahead)
        around = [(i, side, k) for i in (below, near, gx) for k in (0, 1)]
        around += [(i, gy, k) for i in (below, near) for k in (0, 1)] + [other]
    else:
        around = [device(dx, dy) for dx in (-1, 0, 1) for dy in (-1, 0, 1) if (dx, dy) != (0, 0)]
    for to in around:
        pl.semaphore_signal(barrier, inc=1, device_id=to, device_id_type=MESH)
    for copy in local:
        copy.start()
    if not pair:
        pl.semaphore_wait(barrier, len(around))

    def remote(src, dst, send, recv, to):
        copy = pltpu.make_async_remote_copy(
            src_ref=src, dst_ref=dst, send_sem=send, recv_sem=recv,
            device_id=to, device_id_type=MESH)
        copy.start()
        return copy

    moved = []
    shape = (gzn, ny, 128)
    row = lax.broadcasted_iota(jnp.int32, shape, 1)
    lane = lax.broadcasted_iota(jnp.int32, shape, 2)
    rates_copy.wait()
    rate = [rates[index] for index in range(19)]
    sent = list(moved)
    leaving = []

    def arrived(index):
        local[index].wait()

    def shifted(plane, halo, velocity):
        cx, cy, cz = velocity
        value = plane()
        if cy:
            value = jnp.where(row == (0 if cy > 0 else ny - 1),
                              jnp.broadcast_to(halo(), shape), pltpu.roll(value, cy % ny, 1))
        if cz:
            turned = pltpu.roll(value, cz % 128, 2)
            if cz > 0:
                swapped = jnp.concatenate([turned[-1:], turned[:-1]], axis=0)
            else:
                swapped = jnp.concatenate([turned[1:], turned[:1]], axis=0)
            value = jnp.where(lane == (0 if cz > 0 else 127), swapped, turned)
        return value

    def source(t, p, x, is_flag):
        cx, cy, cz = VELOCITY[p]
        sx = x - cx
        outside = sx < 0 or sx >= nx
        xd, yd = (0 if cx > 0 else 1), (0 if cy > 0 else 1)

        def plane():
            if outside:
                return xr[t, xd, 5 if is_flag else X_OUT[xd].index(p)]
            return flag[sx] if is_flag else relaxed[p, sx]

        def halo():
            if outside:
                return er[t, EDGE.index(p), 1 if is_flag else 0]
            return yr[t, yd, 5 if is_flag else Y_OUT[yd].index(p), sx]

        return shifted(plane, halo, (cx, cy, cz))

    def first_step():
        lower = gz == 0
        local[nx].wait()
        flags = [iraw[x].astype(jnp.float32) for x in range(nx)]
        part = lambda value, h: value[h * ny : (h + 1) * ny]
        line = lambda value, at: value[at : at + 1]
        feed = {(0, 1): ny - 1, (0, 0): 2 * ny - 1, (1, 0): ny, (1, 1): 0}

        def put_y(k, x, d, value):
            ys0[0, d, k, x] = line(value, feed[d, d])
            ys0[1, d, k, x] = line(value, feed[d, 1 - d])

        for x in range(nx):
            flag[x, gz] = jnp.where(lower, part(flags[x], 0), part(flags[x], 1))
            fsend[x] = jnp.where(lower, part(flags[x], 1), part(flags[x], 0))
            for d in (0, 1):
                put_y(5, x, d, flags[x])
        for h in (0, 1):
            xs0[h, 0, 5] = part(flags[nx - 1], h)
            xs0[h, 1, 5] = part(flags[0], h)
            for e, p in enumerate(EDGE):
                cx, cy, _ = VELOCITY[p]
                es0[h, e, 1] = line(flags[nx - 1 if cx > 0 else 0], feed[0 if cy > 0 else 1, h])

        def one(place, x):
            arrived(place)
            values = collide([raw[index, x] for index in range(19)], rate)
            for index in range(19):
                low, high = part(values[index], 0), part(values[index], 1)
                relaxed[index, x, gz] = jnp.where(lower, low, high)
                osend[index, x] = jnp.where(lower, high, low)
            for d in (0, 1):
                for k, p in enumerate(Y_OUT[d]):
                    put_y(k, x, d, values[p])
            return values

        faces = {x: one(place, x) for place, x in enumerate(order[:2])}
        for h in (0, 1):
            for e, p in enumerate(EDGE):
                cx, cy, _ = VELOCITY[p]
                es0[h, e, 0] = line(faces[nx - 1 if cx > 0 else 0][p], feed[0 if cy > 0 else 1, h])
            for k in range(5):
                xs0[h, 0, k] = part(faces[nx - 1][X_OUT[0][k]], h)
                xs0[h, 1, k] = part(faces[0][X_OUT[1][k]], h)
        for place, x in enumerate(order[2:]):
            one(place + 2, x)
        pl.semaphore_wait(barrier, len(around))
        e_copies, x_copies, y_copies, r_copies = [], [], [], []
        for h in (0, 1):
            for e, p in enumerate(EDGE):
                cx, cy, _ = VELOCITY[p]
                to_y = gy if (cy > 0) == (h == 1) else (ahead if cy > 0 else back)
                e_copies.append(remote(es0.at[h, e], er.at[0, e, :, gz], e0_send.at[h, e],
                                       e0_recv.at[gz, e], (near if cx > 0 else below, to_y, h)))
        wrap = jnp.where(gx == 0, 1, 0)
        for far in (wrap, 1 - wrap):
            for h in (0, 1):
                x_copies.append(remote(
                    xs0.at[h, far], xr.at[0, far, :, gz], x0_send.at[h, far],
                    x0_recv.at[gz, far], (jnp.where(far == 0, near, below), gy, h)))
        for d, to in ((0, (gx, ahead, 0)), (1, (gx, back, 1))):
            y_copies.append(remote(ys0.at[0, d], yr.at[0, d, :, :, gz], y0_send.at[d],
                                   y0_recv.at[gz], to))
        y_copies.append(remote(ys0.at[1, gz], yr.at[0, gz, :, :, gz], y0_send.at[2],
                               y0_recv.at[2], other))
        yr[0, 1 - gz, :, :, gz] = ys0[1, 1 - gz]
        r_copies.append(remote(fsend, flag.at[:, gz], in_send.at[nx], in_recv.at[nx], other))
        r_copies.append(remote(osend, relaxed.at[:, :, gz], in_send.at[0], in_recv.at[0], other))

        def faces_in():
            for d in (0, 1):
                for k in (0, 1):
                    pltpu.make_async_remote_copy(
                        src_ref=xs0.at[k, d], dst_ref=xr.at[0, d, :, k], send_sem=x0_send.at[k, d],
                        recv_sem=x0_recv.at[k, d], device_id=other,
                        device_id_type=MESH).wait_recv()
            for e in range(4):
                for k in (0, 1):
                    pltpu.make_async_remote_copy(
                        src_ref=es0.at[k, e], dst_ref=er.at[0, e, :, k], send_sem=e0_send.at[k, e],
                        recv_sem=e0_recv.at[k, e], device_id=other,
                        device_id_type=MESH).wait_recv()

        def rows_in():
            for k in (0, 1):
                pltpu.make_async_remote_copy(
                    src_ref=ys0.at[0, 0], dst_ref=yr.at[0, gz, :, :, k], send_sem=y0_send.at[0],
                    recv_sem=y0_recv.at[k], device_id=other, device_id_type=MESH).wait_recv()
            pltpu.make_async_remote_copy(
                src_ref=ys0.at[1, gz], dst_ref=yr.at[0, 1 - gz, :, :, 1 - gz],
                send_sem=y0_send.at[2], recv_sem=y0_recv.at[2], device_id=other,
                device_id_type=MESH).wait_recv()
            for place, x in enumerate([nx, 0]):
                pltpu.make_async_remote_copy(
                    src_ref=fsend if place == 0 else osend,
                    dst_ref=flag.at[:, 1 - gz] if place == 0 else relaxed.at[:, :, 1 - gz],
                    send_sem=in_send.at[x], recv_sem=in_recv.at[x], device_id=other,
                    device_id_type=MESH).wait_recv()

        for copy in r_copies:
            first_sends.append(copy)
        sent.extend(e_copies + x_copies + y_copies)
        return rows_in, faces_in

    first_sends = []
    rows_in = faces_in = None
    if pair:
        rows_in, faces_in = first_step()
    for t in range(STEPS):
        last = t == STEPS - 1
        if t == 0 and not pair:
            arrived(nx)
            for x in range(nx):
                flag[x] = iflag[x].astype(jnp.float32)
                for d, at in ((0, ny - 1), (1, 0)):
                    ys[0, d, 5, x] = flag[x, :, at : at + 1, :]
            xs[0, 0, 5] = flag[nx - 1]
            xs[0, 1, 5] = flag[0]
            for e, p in enumerate(EDGE):
                cx, cy, _ = VELOCITY[p]
                at = ny - 1 if cy > 0 else 0
                es[0, e, 1] = flag[nx - 1 if cx > 0 else 0, :, at : at + 1, :]
        count = 6 if t == 0 else 5
        ecount = 2 if t == 0 else 1
        x_copies, e_copies, y_copies = [], [], []
        for place, x in enumerate(order if t or not pair else []):
            if t == 0:
                arrived(place)
            values = collide([held[index, x] for index in range(19)], rate)
            for index in range(19):
                relaxed[index, x] = values[index]
            for d, at in ((0, ny - 1), (1, 0)):
                for k, p in enumerate(Y_OUT[d]):
                    ys[t, d, k, x] = values[p][:, at : at + 1, :]
            d = {nx - 1: 0, 0: 1}.get(x)
            if d is not None:
                for e, p in enumerate(EDGE):
                    cx, cy, _ = VELOCITY[p]
                    if (cx > 0) == (d == 0):
                        at = ny - 1 if cy > 0 else 0
                        es[t, e, 0] = values[p][:, at : at + 1, :]
                        e_copies.append(remote(
                            es.at[t, e, pl.ds(0, ecount)], er.at[t, e, pl.ds(0, ecount)],
                            e_send.at[t, e], e_recv.at[t, e], device(cx, cy)))
                for k, p in enumerate(X_OUT[d]):
                    xs[t, d, k] = values[p]
            if place == 1:
                wrap = jnp.where(gx == 0, 1, 0)
                for far in (wrap, 1 - wrap):
                    x_copies.append(remote(
                        xs.at[t, far, pl.ds(0, count)], xr.at[t, far, pl.ds(0, count)],
                        x_send.at[t, far], x_recv.at[t, far], device(1 - 2 * far, 0)))
        for d in (0, 1) if t or not pair else ():
            y_copies.append(remote(
                ys.at[t, d, pl.ds(0, count)], yr.at[t, d, pl.ds(0, count)],
                y_send.at[t, d], y_recv.at[t, d], device(0, 1 if d == 0 else -1)))
        while sent:
            sent.pop().wait_send()
        sent += x_copies + e_copies + y_copies
        if last:
            while first_sends:
                first_sends.pop().wait_send()
        for copy in y_copies:
            copy.wait_recv()
        if t == 0 and pair:
            rows_in()
        for place, x in enumerate(order[2:] + order[:2]):
            if place == nx - 2:
                if last:
                    while sent and len(sent) > len(leaving):
                        sent.pop(0).wait_send()
                for copy in x_copies + e_copies:
                    copy.wait_recv()
                if t == 0 and pair:
                    faces_in()
            rock = flag[x] > 0.5
            for p in range(19):
                if p == 0:
                    value = relaxed[0, x]
                else:
                    if t == 0:
                        wall = source(0, p, x, True)
                        blocked[p, x] = wall
                    else:
                        wall = blocked[p, x]
                    value = jnp.where(wall > 0.5, relaxed[OPPOSITE[p], x], source(t, p, x, False))
                value = jnp.where(rock, 0.0, value)
                if not last:
                    held[p, x] = value
                elif pair:
                    first = gz == 0
                    out[p, x, mine, :] = jnp.where(first, value[0], value[1])
                    osend[p, x] = jnp.where(first, value[1], value[0])
                else:
                    out[p, x] = value
            if last and pair:
                copy = remote(osend.at[:, x], out.at[:, x, mine, :],
                              o_send.at[x], o_recv.at[x], other)
                sent.append(copy)
                leaving.append(copy)
                moved.append(copy)
    if pair:
        for copy in moved:
            copy.wait_recv()
    for copy in sent:
        copy.wait_send()


def shards(sizes, populations, solid, rates):
    gxn, gyn, gzn, nx, ny = sizes
    pair = gzn == 2
    if not pair:
        populations = lax.all_to_all(
            populations.reshape(19, nx, gzn, ny, 128), "gz", 2, 2, tiled=True)
        solid = lax.all_to_all(solid.reshape(nx, gzn, ny, 128), "gz", 1, 1, tiled=True)
    f32, dma, vmem = jnp.float32, pltpu.SemaphoreType.DMA, pltpu.VMEM
    block = (gzn, ny, 128)
    line = (gzn, 1, 128)
    out = pl.pallas_call(
        functools.partial(kernel, sizes),
        out_shape=jax.ShapeDtypeStruct(populations.shape, f32),
        in_specs=[
            pl.BlockSpec(memory_space=pltpu.HBM),
            pl.BlockSpec(memory_space=pltpu.HBM),
            pl.BlockSpec(memory_space=pltpu.HBM),
        ],
        out_specs=pl.BlockSpec(memory_space=pltpu.VMEM),
        scratch_shapes=[
            vmem((19, nx) + block, f32),
            vmem((19, nx) + block, f32),
            vmem((nx,) + block, f32),
            vmem((19, nx) + block, f32),
            vmem((STEPS, 2, 6) + block, f32),
            vmem((STEPS, 2, 6) + block, f32),
            vmem((STEPS, 2, 6, nx) + line, f32),
            vmem((STEPS, 2, 6, nx) + line, f32),
            vmem((STEPS, 4, 2) + line, f32),
            vmem((STEPS, 4, 2) + line, f32),
            vmem((19, nx, ny, 128), f32),
            vmem((nx,) + block, jnp.int32),
            pltpu.SMEM((19,), f32),
            vmem((19, nx, gzn * ny, 128), f32),
            vmem((nx, gzn * ny, 128), jnp.int32),
            vmem((nx, ny, 128), f32),
            vmem((2, 2, 6, ny, 128), f32),
            vmem((2, 2, 6, nx, 1, 128), f32),
            vmem((2, 4, 2, 1, 128), f32),
            dma((2, 2)),
            dma((2, 2)),
            dma((3,)),
            dma((3,)),
            dma((2, 4)),
            dma((2, 4)),
            dma((nx + 2,)),
            dma((nx + 1,)),
            dma((nx + 1,)),
            dma((STEPS, 2)),
            dma((STEPS, 2)),
            dma((STEPS, 2)),
            dma((STEPS, 2)),
            dma((STEPS, 4)),
            dma((STEPS, 4)),
            dma((nx,)),
            dma((nx,)),
        ],
        compiler_params=pltpu.CompilerParams(
            collective_id=0, has_side_effects=True, vmem_limit_bytes=32 * 1024 * 1024),
    )(populations, solid, rates)
    if not pair:
        out = lax.all_to_all(out, "gz", 2, 2, tiled=True).reshape(19, nx, gzn * ny, 128)
    return out


def solution(mesh):
    gxn, gyn, gzn = mesh.shape["gx"], mesh.shape["gy"], mesh.shape["gz"]

    def run(populations, solid, rates):
        sizes = (gxn, gyn, gzn, populations.shape[1] // gxn, populations.shape[2] // (gyn * gzn))
        in_specs = (P(None, "gx", "gy", "gz"), P("gx", "gy", "gz"), P())
        out_specs = P(None, "gx", "gy", "gz")
        return jax.shard_map(functools.partial(shards, sizes), mesh=mesh, in_specs=in_specs,
                             out_specs=out_specs, check_vma=False)(populations, solid, rates)

    return run
```
